256 devices in a mesh: sub: 8 (over z_hi, x), strip: 32 (over y, z_lo, core).
Axes of the slice: x: 4, y: 4, z: 8 (z_hi: 2, z_lo: 4; z = z_hi * 4 + z_lo), core: 2. Of those that a mesh axis runs over, the one named last changes fastest.
Arguments:
- forcing: float32 [8, 2048, 2048], P('sub', 'strip'), may hold values from -6 to 6
- mult_start: float32 [8, 2048, 2048], P('sub', 'strip'), may hold values from -6 to 6
- incr_start: float32 [8, 2048, 2048], P('sub', 'strip'), may hold values from -6 to 6
- diffusivity: float32 [8, 2048, 2048], P('sub', 'strip'), may hold values from 0.02 to 0.24
- north_corr: bfloat16 [2048, 2048], P('strip'), may hold values from -0.07629126 to 1.07629126
- east_corr: bfloat16 [2048, 2048], replicated, may hold values from -0.07629126 to 1.07629126
Outputs:
- mult_resid: float32 [8, 2048, 2048], P('sub', 'strip')
- grad_resid: float32 [8, 2048, 2048], P('sub', 'strip')
The draws below stay inside these ranges and needn't reach their ends.
All inputs are finite; a program needn't handle non-finite values.
Results may differ from the reference program's by a relative error of at most 0.014.
Values may be sent and summed in bfloat16 or wider, within the bound.
A program may use at most 128 MiB of HBM per device.

```python
import math
import jax
import jax.numpy as jnp
from jax import lax

NX = 2048
NY = 2048
STEPS = 4
ITERS = 2
SUBW = 8


def corr_matrix(key, matrix_order):
    entries = jax.random.normal(key, (matrix_order, matrix_order), jnp.float32)
    entries = jnp.clip(entries, -6.0, 6.0)
    return (jnp.eye(matrix_order, dtype=jnp.float32) + 0.5 * entries / math.sqrt(matrix_order)).astype(jnp.bfloat16)


def draw_north_corr(key, part):
    return corr_matrix(jax.random.fold_in(key, 11), NX)


def draw_east_corr(key, part):
    return corr_matrix(jax.random.fold_in(key, 12), NY)


def shard_levels(rng, shape, cuts, least, high):
    level = 1.0
    for position, blocks in cuts:
        steps = jax.random.uniform(jax.random.fold_in(jax.random.fold_in(rng, 6), position), (blocks,), jnp.float32, least / len(cuts), high / len(cuts))
        level = level * jnp.repeat(jnp.exp(steps), shape[position] // blocks).reshape((-1,) + (1,) * (len(shape) - 1 - position))
    return level


def normal_values(own_key, dims, scale, most, cuts=(), held_as=jnp.bfloat16):
    values = scale * jax.random.normal(own_key, dims, jnp.float32)
    if cuts:
        values = values * shard_levels(own_key, dims, cuts, -0.22, 0.18)
    return jnp.clip(values, -most, most).astype(held_as)


def setup_inputs(seed: int = 0) -> dict:
    arg_keys = jax.random.split(jax.random.key(seed), 7)
    return {
        "forcing": normal_values(arg_keys[0], (SUBW, NX, NY), 1.0, 6.0, ((0, 8), (1, 32)), jnp.float32),
        "mult_start": normal_values(arg_keys[1], (SUBW, NX, NY), 1.0, 6.0, ((0, 8), (1, 32)), jnp.float32),
        "incr_start": normal_values(arg_keys[2], (SUBW, NX, NY), 1.0, 6.0, ((0, 8), (1, 32)), jnp.float32),
        "diffusivity": jnp.clip(0.02 + 0.22 * jax.random.uniform(arg_keys[3], (SUBW, NX, NY), jnp.float32) ** shard_levels(arg_keys[3], (SUBW, NX, NY), ((0, 8), (1, 32)), -0.2, 0.2), 0.02, 0.24),
        "north_corr": draw_north_corr(jax.random.fold_in(arg_keys[6], 71), 0),
        "east_corr": draw_east_corr(jax.random.fold_in(arg_keys[6], 71), 0),
    }


step_weight = 0.5


def laplace(field):
    padded = jnp.pad(field, ((0, 0), (1, 1), (1, 1)))
    return (padded[:, :-2, 1:-1] + padded[:, 2:, 1:-1] + padded[:, 1:-1, :-2]
            + padded[:, 1:-1, 2:] - 4.0 * padded[:, 1:-1, 1:-1])


def propagate(field, diffuse):
    for each_step in range(STEPS):
        field = field + diffuse * laplace(field)
    return field


def adjoint(field, diffuse):
    for each_step in range(STEPS):
        field = field + laplace(diffuse * field)
    return field


def forward_op(increment, diffusivity):
    moved = propagate(increment[:-1], diffusivity[:-1])
    return increment - jnp.concatenate([jnp.zeros_like(increment[:1]), moved], axis=0)


def backward_op(multiplier, diffusivity):
    pulled = adjoint(multiplier[1:], diffusivity[:-1])
    return multiplier - jnp.concatenate([pulled, jnp.zeros_like(multiplier[:1])], axis=0)


def correlate(field, north_corr, east_corr):
    north = north_corr.astype(jnp.float32)
    east = east_corr.astype(jnp.float32)

    def single(sheet):
        lowered = lax.optimization_barrier(sheet.astype(jnp.bfloat16)).astype(jnp.float32)
        north_half = jnp.dot(north, lowered, precision=lax.Precision.HIGHEST)
        north_half = lax.optimization_barrier(north_half.astype(jnp.bfloat16)).astype(jnp.float32)
        return jnp.dot(north_half, east, precision=lax.Precision.HIGHEST)

    return lax.map(single, field)


def reference(forcing, mult_start, incr_start, diffusivity, north_corr, east_corr):
    multiplier = mult_start
    increment = incr_start
    for iteration in range(ITERS):
        multiplier = multiplier + step_weight * (forcing - correlate(multiplier, north_corr, east_corr)
                                                 - forward_op(increment, diffusivity))
        increment = increment + step_weight * backward_op(multiplier, diffusivity)
    mult_resid = forcing - correlate(multiplier, north_corr, east_corr) - forward_op(increment, diffusivity)
    grad_resid = backward_op(multiplier, diffusivity)
    return mult_resid, grad_resid
```

```python
import functools

import jax
import jax.numpy as jnp
from jax import lax
from jax.experimental import pallas as pl
from jax.experimental.pallas import tpu as pltpu
from jax.sharding import PartitionSpec as P

STEPS = 4
ITERS = 2
PHASES = ITERS + 1
MESH = pl.DeviceIdType.MESH
F32, BF16 = jnp.float32, jnp.bfloat16

ROWS, WIDE, CHUNKS, LANES = 64, 80, 16, 128
HALO = 8
GATHER_PARTS = ((0, 1024, "zy"), (1024, 1024, "yz"))

DIFF, INCR, MULT = 0, 1, 2


def kernel(forcing, mult_in, incr_in, diff_in, north, east, mult_out, grad_out,
           north_all, east_all, low_land, half_land, half_mine, strip_land, rim_land, strip_mine, rim_mine,
           work, diff_prev, diff_own, incr_prev, incr_own, mult, force, half_flat, model,
           load_sem, gather_send, gather_recv, there_send, there_recv, core_sem, back_send, back_recv,
           swap_send, swap_recv, out_sem):
    sub, strip = lax.axis_index("sub"), lax.axis_index("strip")
    x, z_hi = lax.rem(sub, 4), lax.div(sub, 4)
    y, z, core = lax.div(strip, 8), lax.rem(lax.div(strip, 2), 4), lax.rem(strip, 2)
    chip, z_all = y * 4 + z, z_hi * 4 + z

    def device(x_at, y_at, z_at):
        return (lax.div(z_at, 4) * 4 + x_at, y_at * 8 + lax.rem(z_at, 4) * 2 + core)

    def along(dim, step):
        if dim == "y":
            return device(x, lax.rem(y + step + 4, 4), z_all)
        return device(x, y, lax.rem(z_all + step + 8, 8))

    peer = (sub, strip + 1 - 2 * core)

    def plane(offset):
        to = lax.rem(chip + offset, 16)
        return to, (sub, to * 2 + core)

    def remote(src, dst, send, recv, to):
        return pltpu.make_async_remote_copy(
            src_ref=src, dst_ref=dst, send_sem=send, recv_sem=recv, device_id=to, device_id_type=MESH
        )

    first, last = sub == 0, sub == 7
    top, bottom = strip == 0, strip == 31

    def load(source, target, sem):
        for j in range(CHUNKS):
            pltpu.make_async_copy(source.at[:, pl.ds(LANES * j, LANES)], target.at[j], sem).start()

    def loaded(target, sem):
        pltpu.make_async_copy(target, target, sem).wait()

    load(mult_in.at[0], mult, load_sem.at[0])
    load(incr_in.at[0], incr_own, load_sem.at[1])
    load(diff_in.at[0], force, load_sem.at[2])
    own_north = pltpu.make_async_copy(north, north_all.at[chip], load_sem.at[3])
    own_north.start()
    own_east = pltpu.make_async_copy(east, east_all, load_sem.at[4])
    own_east.start()
    rim_land[...] = jnp.zeros_like(rim_land)
    for ref in (work, diff_prev, diff_own):
        ref[0] = jnp.zeros((WIDE, LANES), F32)
        ref[CHUNKS + 1] = jnp.zeros((WIDE, LANES), F32)

    barrier = pltpu.get_barrier_semaphore()

    def greet(to):
        pl.semaphore_signal(barrier, inc=1, device_id=to, device_id_type=MESH)

    @pl.loop(1, 16)
    def _(offset):
        greet(plane(offset)[1])

    greet(peer)
    for step in (-1, 1):
        greet(along("z", step))
    near = [
        (-1, 0, ~first), (1, 0, ~last),
        (-1, -1, ~first & ~top), (-1, 1, ~first & ~bottom),
        (1, -1, ~last & ~top), (1, 1, ~last & ~bottom),
        (0, -1, ~top), (0, 1, ~bottom),
    ]
    for d_sub, d_strip, there in near:
        @pl.when(there)
        def _(d_sub=d_sub, d_strip=d_strip):
            greet((sub + d_sub, strip + d_strip))
    expected = 18
    for _, _, there in near:
        expected = expected + there.astype(jnp.int32)
    pl.semaphore_wait(barrier, expected)

    gather_sends = []

    def part_copy(part, piece, half, src, to, recv_at, sends):
        start, size, _ = GATHER_PARTS[part]
        if half is not None:
            start, size = start + half * (size // 2), size // 2
        columns = pl.ds(start, size)
        source = (north if src else north_all.at[piece]).at[:, columns]
        return remote(source, north_all.at[piece, :, columns], gather_send.at[sends], gather_recv.at[recv_at], to)

    def slot(part, rel_a, rel_b, half=0):
        return ((part * 4 + rel_a) * 4 + rel_b) * 2 + half

    def piece_of(part, rel_a, rel_b):
        rel_z, rel_y = (rel_a, rel_b) if GATHER_PARTS[part][2] == "zy" else (rel_b, rel_a)
        return lax.rem(y + rel_y, 4) * 4 + lax.rem(z + rel_z, 4)

    def gather_send_piece(part, rel_a, rel_b, dim_at, step, half=None):
        dim = GATHER_PARTS[part][2][dim_at]
        to_a, to_b = (rel_a, rel_b)
        if dim_at == 0:
            to_a = (rel_a - step) % 4
        else:
            to_b = (rel_b - step) % 4
        copy = part_copy(
            part, piece_of(part, rel_a, rel_b), half, (rel_a, rel_b) == (0, 0), along(dim, step),
            slot(part, to_a, to_b, half or 0), len(gather_sends),
        )
        copy.start()
        gather_sends.append(copy)

    def gather_wait(part, rel_a, rel_b, half=None):
        part_copy(part, piece_of(part, rel_a, rel_b), half, False, peer, slot(part, rel_a, rel_b, half or 0), 0).wait_recv()

    parts = range(len(GATHER_PARTS))
    for part in parts:
        for dim_at in (0, 1):
            for step in (1, -1):
                gather_send_piece(part, 0, 0, dim_at, step)

    def gather_first_ring():
        for rel, step in ((3, 1), (1, -1)):
            for part in parts:
                gather_wait(part, rel, 0)
                gather_send_piece(part, rel, 0, 0, step, half=0 if step == 1 else 1)
                gather_send_piece(part, rel, 0, 1, 1)
                gather_send_piece(part, rel, 0, 1, -1)

    def gather_own_second():
        for rel, step in ((3, 1), (1, -1)):
            for part in parts:
                gather_wait(part, 0, rel)
                gather_send_piece(part, 0, rel, 1, step, half=0 if step == 1 else 1)

    def gather_far():
        for part in parts:
            gather_wait(part, 2, 0, 0)
            gather_wait(part, 2, 0, 1)
            gather_send_piece(part, 2, 0, 1, 1)
            gather_send_piece(part, 2, 0, 1, -1)

    def gather_rest():
        for rel_a in (3, 1, 2):
            for rel, step in ((3, 1), (1, -1)):
                for part in parts:
                    gather_wait(part, rel_a, rel)
                    gather_send_piece(part, rel_a, rel, 1, step, half=0 if step == 1 else 1)
        for rel_a in (0, 3, 1, 2):
            for part in parts:
                gather_wait(part, rel_a, 2, 0)
                gather_wait(part, rel_a, 2, 1)

    def swap_copies(which):
        copies = []
        for at, d_sub in ((0, 1), (1, -1)):
            if which < MULT and d_sub == -1:
                continue
            sent = ~last if d_sub == 1 else ~first
            heard = ~first if d_sub == 1 else ~last
            copies.append((remote(
                strip_mine.at[which], strip_land.at[which, at], swap_send.at[which, at],
                swap_recv.at[which, at], (sub + d_sub, strip)), sent, heard))
        for at, d_sub in ((0, 1), (1, 0), (2, -1)):
            if (which == INCR and d_sub == 0) or (which < MULT and d_sub == -1):
                continue
            sub_sent = {1: ~last, 0: first | ~first, -1: ~first}[d_sub]
            sub_heard = {1: ~first, 0: first | ~first, -1: ~last}[d_sub]
            for edge, d_strip in ((0, -1), (1, 1)):
                sent = sub_sent & (~top if d_strip == -1 else ~bottom)
                heard = sub_heard & (~bottom if d_strip == -1 else ~top)
                number = 2 + 2 * at + edge
                copies.append((remote(
                    rim_mine.at[which, edge], rim_land.at[which, at, 1 - edge], swap_send.at[which, number],
                    swap_recv.at[which, number], (sub + d_sub, strip + d_strip)), sent, heard))
        return copies

    def swap_start(which):
        for copy, sent, _ in swap_copies(which):
            pl.when(sent)(copy.start)

    def swap_wait(which, wanted):
        for copy, _, heard in swap_copies(which):
            if wanted(copy):
                pl.when(heard)(copy.wait_recv)

    def swap_wait_number(which, numbers):
        copies = swap_copies(which)
        order = ([0, 1] if which >= MULT else [0]) + [
            2 + 2 * at + edge
            for at, d_sub in ((0, 1), (1, 0), (2, -1))
            if not ((which == INCR and d_sub == 0) or (which < MULT and d_sub == -1))
            for edge in (0, 1)
        ]
        for number, (copy, _, heard) in zip(order, copies, strict=True):
            if number in numbers:
                pl.when(heard)(copy.wait_recv)

    FROM_BEFORE, FROM_SAME, FROM_AFTER = (0, 2, 3), (4, 5), (1, 6, 7)

    def pack(which, field):
        @pl.loop(0, CHUNKS // 2)
        def _(pair):
            left, right = field[2 * pair], field[2 * pair + 1]
            strip_mine[which, 2 * pair] = left.astype(BF16)
            strip_mine[which, 2 * pair + 1] = right.astype(BF16)
            rim_mine[which, 0, pair] = jnp.concatenate([left[:HALO], right[:HALO]], axis=0).astype(BF16)
            rim_mine[which, 1, pair] = jnp.concatenate([left[-HALO:], right[-HALO:]], axis=0).astype(BF16)

    def widened(which, source, chunk_rows, pair):
        above = rim_land[which, source, 0, pair].astype(F32)
        below = rim_land[which, source, 1, pair].astype(F32)
        return [
            jnp.concatenate(
                [above[h * HALO:(h + 1) * HALO], chunk_rows(2 * pair + h), below[h * HALO:(h + 1) * HALO]], axis=0
            )
            for h in (0, 1)
        ]

    def each_wide(which, source, chunk_rows, put):
        @pl.loop(0, CHUNKS // 2)
        def _(pair):
            for h, value in enumerate(widened(which, source, chunk_rows, pair)):
                put(2 * pair + h, value)

    def landed(which, source):
        return lambda j: strip_land[which, source, j].astype(F32)

    lane = lax.broadcasted_iota(jnp.int32, (WIDE, LANES), 1)
    leftmost, rightmost = lane == 0, lane == LANES - 1

    def spread(before, now, now_left, after_left):
        now_right = pltpu.roll(now, 1, 1)
        total = (
            jnp.where(leftmost, before, now_right) + jnp.where(rightmost, after_left, now_left)
            + pltpu.roll(now, 1, 0) + pltpu.roll(now, WIDE - 1, 0) - 4.0 * now
        )
        return total, now_right

    def run_model(diff):
        @pl.loop(0, STEPS)
        def _(step):
            def body(j, carry):
                before, now, now_left = carry
                after = work[j + 1]
                after_left = pltpu.roll(after, LANES - 1, 1)
                total, now_right = spread(before, now, now_left, after_left)
                work[j] = now + diff[j] * total
                return now_right, after, after_left
            start = work[1]
            lax.fori_loop(1, CHUNKS + 1, body, (jnp.zeros((WIDE, LANES), F32), start, pltpu.roll(start, LANES - 1, 1)))

    def run_adjoint(diff):
        @pl.loop(0, STEPS)
        def _(step):
            def body(j, carry):
                before, now, now_left, field = carry
                later = work[j + 1]
                after = diff[j + 1] * later
                after_left = pltpu.roll(after, LANES - 1, 1)
                total, now_right = spread(before, now, now_left, after_left)
                work[j] = field + total
                return now_right, after, after_left, later
            field = work[1]
            start = diff[1] * field
            lax.fori_loop(
                1, CHUNKS + 1, body, (jnp.zeros((WIDE, LANES), F32), start, pltpu.roll(start, LANES - 1, 1), field)
            )

    def put_work(j, value):
        work[j + 1] = value

    row = lax.broadcasted_iota(jnp.int32, (WIDE, LANES), 0)
    inside = ~((row < HALO) & top) & ~((row >= HALO + ROWS) & bottom)

    def there_copy(phase, offset):
        to, at = plane(offset)
        return remote(
            strip_mine.at[MULT - 1 + phase if phase else 4, to], low_land.at[phase, chip, core],
            there_send.at[phase, offset], there_recv.at[phase, offset], at)

    def there_start(phase):
        @pl.loop(1, 16)
        def _(offset):
            there_copy(phase, offset).start()
        low_land[phase, chip, core] = strip_mine[MULT - 1 + phase if phase else 4, chip]

    def core_copy(phase):
        mine = low_land.at[phase, :, core]
        return remote(mine, mine, core_sem.at[phase, 0], core_sem.at[phase, 1], peer)

    def there_wait(phase):
        @pl.loop(1, 16)
        def _(offset):
            there_copy(phase, offset).wait_recv()
        core_copy(phase).start()

    def back_copy(phase, offset):
        to, at = plane(offset)
        return remote(
            half_mine.at[phase, to], half_land.at[phase, chip], back_send.at[phase, offset],
            back_recv.at[phase, offset], at)

    def north_product(phase):
        core_copy(phase).wait_recv()

        @pl.loop(0, 4)
        def _(quarter):
            blocks = north_all[pl.ds(4 * quarter, 4)].reshape(4 * ROWS, 2048)
            columns = low_land[phase].reshape(2048, LANES)
            product = jnp.dot(blocks, columns, preferred_element_type=F32).astype(BF16)
            half_mine[phase, pl.ds(4 * quarter, 4)] = product.reshape(4, ROWS, LANES)

        @pl.loop(1, 16)
        def _(offset):
            back_copy(phase, offset).start()
        half_land[phase, chip] = half_mine[phase, chip]

    def east_product(phase, finish):
        @pl.loop(1, 16)
        def _(offset):
            back_copy(phase, offset).wait_recv()
        for j in range(CHUNKS):
            half_flat[:, LANES * j:LANES * (j + 1)] = half_land[phase, j]

        @pl.loop(0, 8)
        def _(pair):
            columns = pl.ds(pl.multiple_of(256 * pair, 256), 256)
            product = jnp.dot(half_flat[...], east_all[:, columns], preferred_element_type=F32)
            finish(2 * pair, product[:, :LANES])
            finish(2 * pair + 1, product[:, LANES:])

    loaded(mult, load_sem.at[0])

    @pl.loop(0, CHUNKS)
    def _(j):
        strip_mine[4, j] = mult[j].astype(BF16)

    there_start(0)
    loaded(force, load_sem.at[2])
    pack(DIFF, force)
    swap_start(DIFF)
    loaded(incr_own, load_sem.at[1])
    pack(INCR, incr_own)
    swap_start(INCR)
    gather_first_ring()
    gather_own_second()
    gather_far()
    there_wait(0)
    swap_wait_number(DIFF, FROM_SAME)

    def put_own(j, value):
        diff_own[j + 1] = value

    each_wide(DIFF, 1, lambda j: force[j], put_own)
    load(forcing.at[0], force, load_sem.at[2])
    swap_wait_number(DIFF, FROM_BEFORE)

    def put_prev(j, value):
        diff_prev[j + 1] = value

    each_wide(DIFF, 0, landed(DIFF, 0), put_prev)
    swap_wait_number(INCR, FROM_BEFORE)

    def put_incr(j, value):
        incr_prev[j] = value
        work[j + 1] = value

    each_wide(INCR, 0, landed(INCR, 0), put_incr)
    own_north.wait()
    gather_rest()
    north_product(0)
    run_model(diff_prev)

    def keep_model():
        @pl.loop(0, CHUNKS)
        def _(j):
            moved = jnp.where(first, 0.0, work[j + 1, HALO:HALO + ROWS])
            model[j] = force[j] - incr_own[j] + moved

    loaded(force, load_sem.at[2])
    keep_model()
    own_east.wait()

    def update(j, product):
        mult[j] = mult[j] + 0.5 * (model[j] - product)

    east_product(0, update)

    for phase in range(1, PHASES):
        which = MULT - 1 + phase
        final = phase == PHASES - 1
        pack(which, mult)
        there_start(phase)
        swap_start(which)
        swap_wait_number(which, FROM_SAME)
        each_wide(which, 1, lambda j: mult[j], put_work)
        run_adjoint(diff_prev)
        there_wait(phase)

        @pl.loop(0, CHUNKS)
        def _(j):
            incr_prev[j] = incr_prev[j] - 0.5 * work[j + 1]

        north_product(phase)
        swap_wait_number(which, FROM_BEFORE)

        def put_before(j, value):
            value = jnp.where(inside, incr_prev[j] + 0.5 * value, 0.0)
            incr_prev[j] = value
            work[j + 1] = value

        each_wide(which, 0, landed(which, 0), put_before)
        run_model(diff_prev)

        @pl.loop(0, CHUNKS)
        def _(j):
            model[j] = force[j] + jnp.where(first, 0.0, work[j + 1, HALO:HALO + ROWS])

        swap_wait_number(which, FROM_AFTER)
        each_wide(which, 2, landed(which, 1), put_work)
        run_adjoint(diff_own)

        @pl.loop(0, CHUNKS)
        def _(j):
            grad = mult[j] - jnp.where(last, 0.0, work[j + 1, HALO:HALO + ROWS])
            incr = incr_own[j] + 0.5 * grad
            incr_own[j] = incr
            model[j] = model[j] - incr
            if final:
                work[j + 1, HALO:HALO + ROWS] = grad

        def stored(source, target, sem):
            return [
                pltpu.make_async_copy(source(j), target.at[0, :, pl.ds(LANES * j, LANES)], sem) for j in range(CHUNKS)
            ]

        if not final:
            east_product(phase, update)
        else:
            for copy in stored(lambda j: work.at[j + 1, pl.ds(HALO, ROWS)], grad_out, out_sem.at[0]):
                copy.start()

            def finish(j, product):
                model[j] = model[j] - product

            east_product(phase, finish)
            for copy in stored(lambda j: model.at[j], mult_out, out_sem.at[1]):
                copy.start()

    for copy in gather_sends:
        copy.wait_send()
    for phase in range(PHASES):
        @pl.loop(1, 16)
        def _(offset, phase=phase):
            there_copy(phase, offset).wait_send()
            back_copy(phase, offset).wait_send()
        core_copy(phase).wait_send()
    for which in (DIFF, INCR, MULT, MULT + 1):
        for copy, sent, _ in swap_copies(which):
            pl.when(sent)(copy.wait_send)
    pltpu.make_async_copy(model, model, out_sem.at[0]).wait()
    pltpu.make_async_copy(model, model, out_sem.at[1]).wait()


def local(forcing, mult_start, incr_start, diffusivity, north_corr, east_corr):
    any_space = pl.BlockSpec(memory_space=pl.ANY)
    dma = pltpu.SemaphoreType.DMA
    strip = (CHUNKS, ROWS, LANES)
    wide = (CHUNKS, WIDE, LANES)
    padded = (CHUNKS + 2, WIDE, LANES)
    pieces = len(GATHER_PARTS)
    out = jax.ShapeDtypeStruct((1, ROWS, 2048), F32)
    return pl.pallas_call(
        kernel,
        out_shape=(out, out),
        in_specs=[any_space] * 6,
        out_specs=(any_space, any_space),
        scratch_shapes=[
            pltpu.VMEM((16, ROWS, 2048), BF16),
            pltpu.VMEM((2048, 2048), BF16),
            pltpu.VMEM((PHASES, 16, 2, ROWS, LANES), BF16),
            pltpu.VMEM((PHASES,) + strip, BF16),
            pltpu.VMEM((PHASES,) + strip, BF16),
            pltpu.VMEM((4, 2) + strip, BF16),
            pltpu.VMEM((4, 3, 2, CHUNKS // 2, 2 * HALO, LANES), BF16),
            pltpu.VMEM((5,) + strip, BF16),
            pltpu.VMEM((4, 2, CHUNKS // 2, 2 * HALO, LANES), BF16),
            pltpu.VMEM(padded, F32),
            pltpu.VMEM(padded, F32),
            pltpu.VMEM(padded, F32),
            pltpu.VMEM(wide, F32),
            pltpu.VMEM(strip, F32),
            pltpu.VMEM(strip, F32),
            pltpu.VMEM(strip, F32),
            pltpu.VMEM((ROWS, 2048), BF16),
            pltpu.VMEM(strip, F32),
            dma((5,)),
            dma((pieces * 20,)),
            dma((pieces * 32,)),
            dma((PHASES, 16)),
            dma((PHASES, 16)),
            dma((PHASES, 2)),
            dma((PHASES, 16)),
            dma((PHASES, 16)),
            dma((4, 8)),
            dma((4, 8)),
            dma((2,)),
        ],
        compiler_params=pltpu.CompilerParams(
            collective_id=0, has_side_effects=True, vmem_limit_bytes=48 * 2**20
        ),
    )(forcing, mult_start, incr_start, diffusivity, north_corr, east_corr)


def solution(mesh):
    rows = P("sub", "strip", None)
    return jax.shard_map(
        local,
        mesh=mesh,
        in_specs=(rows, rows, rows, rows, P("strip", None), P()),
        out_specs=(rows, rows),
        check_vma=False,
    )
```

```python
import functools

import jax
import jax.numpy as jnp
from jax import lax
from jax.experimental import pallas as pl
from jax.experimental.pallas import tpu as pltpu
from jax.sharding import PartitionSpec as P

STEPS = 4
ITERS = 2
PHASES = ITERS + 1
MESH = pl.DeviceIdType.MESH
F32, BF16 = jnp.float32, jnp.bfloat16

ROWS, WIDE, CHUNKS, LANES = 64, 80, 16, 128
HALO = 8
GATHER_PARTS = ((0, 1024, "zy"), (1024, 1024, "yz"))

DIFF, INCR, MULT = 0, 1, 2


def kernel(forcing, mult_in, incr_in, diff_in, north, east, mult_out, grad_out,
           north_all, east_all, low_land, half_land, half_mine, strip_land, rim_land, strip_mine, rim_mine,
           work, diff_prev, diff_own, incr_prev, incr_own, mult, force, model, north_sum, east_sum, relay_out, relay_in,
           load_sem, gather_send, gather_recv, there_send, there_recv, core_send, core_recv, back_send, back_recv,
           swap_send, swap_recv, relay_send, relay_recv, out_sem):
    sub, strip = lax.axis_index("sub"), lax.axis_index("strip")
    x, z_hi = lax.rem(sub, 4), lax.div(sub, 4)
    y, z, core = lax.div(strip, 8), lax.rem(lax.div(strip, 2), 4), lax.rem(strip, 2)
    chip, z_all = y * 4 + z, z_hi * 4 + z

    def device(x_at, y_at, z_at):
        return (lax.div(z_at, 4) * 4 + x_at, y_at * 8 + lax.rem(z_at, 4) * 2 + core)

    def along(dim, step):
        if dim == "y":
            return device(x, lax.rem(y + step + 4, 4), z_all)
        return device(x, y, lax.rem(z_all + step + 8, 8))

    peer = (sub, strip + 1 - 2 * core)

    def plane(offset):
        to = lax.rem(chip + offset, 16)
        return to, (sub, to * 2 + core)

    def remote(src, dst, send, recv, to):
        return pltpu.make_async_remote_copy(
            src_ref=src, dst_ref=dst, send_sem=send, recv_sem=recv, device_id=to, device_id_type=MESH
        )

    first, last = sub == 0, sub == 7
    top, bottom = strip == 0, strip == 31
    hub = jnp.where(z_hi == 0, 3, 4)
    is_hub = sub == hub
    across = (lax.rem(sub + 4, 8), strip)

    def load(source, target, sem):
        for j in range(CHUNKS):
            pltpu.make_async_copy(source.at[:, pl.ds(LANES * j, LANES)], target.at[j], sem).start()

    def loaded(target, sem):
        pltpu.make_async_copy(target, target, sem).wait()

    load(mult_in.at[0], mult, load_sem.at[0])
    load(incr_in.at[0], incr_own, load_sem.at[1])
    load(diff_in.at[0], force, load_sem.at[2])
    own_north = pltpu.make_async_copy(north, north_all.at[chip], load_sem.at[3])
    own_north.start()
    own_east = pltpu.make_async_copy(east, east_all, load_sem.at[4])
    own_east.start()
    rim_land[...] = jnp.zeros_like(rim_land)
    for ref in (work, diff_prev, diff_own):
        ref[0] = jnp.zeros((WIDE, LANES), F32)
        ref[CHUNKS + 1] = jnp.zeros((WIDE, LANES), F32)

    barrier = pltpu.get_barrier_semaphore()

    def greet(to):
        pl.semaphore_signal(barrier, inc=1, device_id=to, device_id_type=MESH)

    for offset in range(1, 16):
        greet(plane(offset)[1])
    greet(peer)
    greet(across)
    for step in (-1, 1):
        greet(along("z", step))
    near = [
        (-1, 0, ~first), (1, 0, ~last),
        (-1, -1, ~first & ~top), (-1, 1, ~first & ~bottom),
        (1, -1, ~last & ~top), (1, 1, ~last & ~bottom),
        (0, -1, ~top), (0, 1, ~bottom),
    ]
    for d_sub, d_strip, there in near:
        @pl.when(there)
        def _(d_sub=d_sub, d_strip=d_strip):
            greet((sub + d_sub, strip + d_strip))
    for part in range(4):
        @pl.when(is_hub & (x != part))
        def _(part=part):
            greet((z_hi * 4 + part, strip))

    @pl.when(~is_hub)
    def _():
        greet((hub, strip))

    expected = 19 + jnp.where(is_hub, 3, 1)
    for _, _, there in near:
        expected = expected + there.astype(jnp.int32)
    pl.semaphore_wait(barrier, expected)

    gather_sends = []

    def part_copy(part, piece, half, src, to, recv_at, sends):
        start, size, _ = GATHER_PARTS[part]
        if half is not None:
            start, size = start + half * (size // 2), size // 2
        columns = pl.ds(start, size)
        source = (north if src else north_all.at[piece]).at[:, columns]
        return remote(source, north_all.at[piece, :, columns], gather_send.at[sends], gather_recv.at[recv_at], to)

    def slot(part, rel_a, rel_b, half=0):
        return ((part * 4 + rel_a) * 4 + rel_b) * 2 + half

    def piece_of(part, rel_a, rel_b):
        rel_z, rel_y = (rel_a, rel_b) if GATHER_PARTS[part][2] == "zy" else (rel_b, rel_a)
        return lax.rem(y + rel_y, 4) * 4 + lax.rem(z + rel_z, 4)

    def gather_send_piece(part, rel_a, rel_b, dim_at, step, half=None):
        dim = GATHER_PARTS[part][2][dim_at]
        to_a, to_b = (rel_a, rel_b)
        if dim_at == 0:
            to_a = (rel_a - step) % 4
        else:
            to_b = (rel_b - step) % 4
        copy = part_copy(
            part, piece_of(part, rel_a, rel_b), half, (rel_a, rel_b) == (0, 0), along(dim, step),
            slot(part, to_a, to_b, half or 0), len(gather_sends),
        )
        copy.start()
        gather_sends.append(copy)

    def gather_wait(part, rel_a, rel_b, half=None):
        part_copy(part, piece_of(part, rel_a, rel_b), half, False, peer, slot(part, rel_a, rel_b, half or 0), 0).wait_recv()

    parts = range(len(GATHER_PARTS))
    for part in parts:
        for dim_at in (0, 1):
            for step in (1, -1):
                gather_send_piece(part, 0, 0, dim_at, step)

    def gather_first_ring():
        for rel, step in ((3, 1), (1, -1)):
            for part in parts:
                gather_wait(part, rel, 0)
                gather_send_piece(part, rel, 0, 0, step, half=0 if step == 1 else 1)
                gather_send_piece(part, rel, 0, 1, 1)
                gather_send_piece(part, rel, 0, 1, -1)

    def gather_own_second():
        for rel, step in ((3, 1), (1, -1)):
            for part in parts:
                gather_wait(part, 0, rel)
                gather_send_piece(part, 0, rel, 1, step, half=0 if step == 1 else 1)

    def gather_far():
        for part in parts:
            gather_wait(part, 2, 0, 0)
            gather_wait(part, 2, 0, 1)
            gather_send_piece(part, 2, 0, 1, 1)
            gather_send_piece(part, 2, 0, 1, -1)

    def gather_rest():
        for rel_a in (3, 1, 2):
            for rel, step in ((3, 1), (1, -1)):
                for part in parts:
                    gather_wait(part, rel_a, rel)
                    gather_send_piece(part, rel_a, rel, 1, step, half=0 if step == 1 else 1)
        for rel_a in (0, 3, 1, 2):
            for part in parts:
                gather_wait(part, rel_a, 2, 0)
                gather_wait(part, rel_a, 2, 1)

    def swap_copies(which):
        copies = []
        for at, d_sub in ((0, 1), (1, -1)):
            if which < MULT and d_sub == -1:
                continue
            sent = ~last & (sub != 3) if d_sub == 1 else ~first & (sub != 4)
            heard = ~first & (sub != 4) if d_sub == 1 else ~last & (sub != 3)
            copies.append((remote(
                strip_mine.at[which], strip_land.at[which, at], swap_send.at[which, at],
                swap_recv.at[which, at], (sub + d_sub, strip)), sent, heard))
        for at, d_sub in ((0, 1), (1, 0), (2, -1)):
            if (which == INCR and d_sub == 0) or (which < MULT and d_sub == -1):
                continue
            sub_sent = {1: ~last, 0: first | ~first, -1: ~first}[d_sub]
            sub_heard = {1: ~first, 0: first | ~first, -1: ~last}[d_sub]
            for edge, d_strip in ((0, -1), (1, 1)):
                sent = sub_sent & (~top if d_strip == -1 else ~bottom)
                heard = sub_heard & (~bottom if d_strip == -1 else ~top)
                number = 2 + 2 * at + edge
                copies.append((remote(
                    rim_mine.at[which, edge], rim_land.at[which, at, 1 - edge], swap_send.at[which, number],
                    swap_recv.at[which, number], (sub + d_sub, strip + d_strip)), sent, heard))
        return copies

    def swap_start(which):
        relay_from_hub(which)
        for copy, sent, _ in swap_copies(which):
            pl.when(sent)(copy.start)

    def swap_wait_number(which, numbers):
        copies = swap_copies(which)
        order = ([0, 1] if which >= MULT else [0]) + [
            2 + 2 * at + edge
            for at, d_sub in ((0, 1), (1, 0), (2, -1))
            if not ((which == INCR and d_sub == 0) or (which < MULT and d_sub == -1))
            for edge in (0, 1)
        ]
        for number, (copy, _, heard) in zip(order, copies, strict=True):
            if number in numbers:
                pl.when(heard)(copy.wait_recv)

    def relay_copies(which):
        up_only = which < MULT
        gives = z_hi == 0 if up_only else z_hi >= 0
        takes = z_hi == 1 if up_only else z_hi >= 0
        land = 0 if up_only else jnp.where(z_hi == 0, 1, 0)
        far_land = 0 if up_only else 1 - land
        quarter = lambda ref, part: ref.at[pl.ds(4 * part, 4)]
        send, recv = relay_send.at[which], relay_recv.at[which]
        outward = [
            (remote(quarter(strip_mine.at[which], part), relay_out.at[which], send.at[part], recv.at[0],
                    (z_hi * 4 + part, strip)), gives & is_hub & (x != part))
            for part in range(4)
        ]
        mine, kept = quarter(strip_mine.at[which], x), relay_out.at[which]
        there, there_kept = quarter(strip_land.at[which, far_land], x), relay_in.at[which]
        far_hub = across[0] == 7 - hub
        over = [
            (remote(mine, there_kept, send.at[4], recv.at[1], across), gives & is_hub),
            (remote(kept, there, send.at[4], recv.at[1], across), gives & ~is_hub & far_hub),
            (remote(kept, there_kept, send.at[4], recv.at[1], across), gives & ~is_hub & ~far_hub),
        ]
        inward = (remote(relay_in.at[which], quarter(strip_land.at[which, land], x), send.at[5], recv.at[2 + x], (hub, strip)),
                  takes & ~is_hub)
        waits = {
            "out": (outward[0][0], gives & ~is_hub),
            "over": (over[0][0], takes),
            "in": [
                (remote(relay_in.at[which], quarter(strip_land.at[which, land], part), send.at[5], recv.at[2 + part], (hub, strip)),
                 takes & is_hub & (x != part))
                for part in range(4)
            ],
        }
        return outward, over, inward, waits

    def relay_from_hub(which):
        outward, over, _, _ = relay_copies(which)
        pl.when(over[0][1])(over[0][0].start)
        for copy, sent in outward:
            pl.when(sent)(copy.start)

    def relay_across(which):
        _, over, _, waits = relay_copies(which)
        copy, heard = waits["out"]
        pl.when(heard)(copy.wait_recv)
        for copy, sent in over[1:]:
            pl.when(sent)(copy.start)

    def relay_to_hub(which):
        _, _, (copy, sent), waits = relay_copies(which)
        arrived, heard = waits["over"]
        pl.when(heard)(arrived.wait_recv)
        pl.when(sent)(copy.start)

    def relay_end(which, hub_sub):
        for copy, heard in relay_copies(which)[3]["in"]:
            pl.when(heard & (sub == hub_sub))(copy.wait_recv)

    def relay_sent(which):
        outward, over, (copy, sent), _ = relay_copies(which)
        for one, was in outward:
            pl.when(was)(one.wait_send)
        gives = over[0][1] | over[1][1] | over[2][1]
        pl.when(gives)(over[0][0].wait_send)
        pl.when(sent)(copy.wait_send)

    FROM_BEFORE, FROM_SAME, FROM_AFTER = (0, 2, 3), (4, 5), (1, 6, 7)

    def pack(which, field):
        for pair in range(CHUNKS // 2):
            left, right = field[2 * pair], field[2 * pair + 1]
            if which < MULT:
                strip_mine[which, 2 * pair] = left.astype(BF16)
                strip_mine[which, 2 * pair + 1] = right.astype(BF16)
            rim_mine[which, 0, pair] = jnp.concatenate([left[:HALO], right[:HALO]], axis=0).astype(BF16)
            rim_mine[which, 1, pair] = jnp.concatenate([left[-HALO:], right[-HALO:]], axis=0).astype(BF16)

    def widened(which, source, chunk_rows, pair):
        above = rim_land[which, source, 0, pair].astype(F32)
        below = rim_land[which, source, 1, pair].astype(F32)
        return [
            jnp.concatenate(
                [above[h * HALO:(h + 1) * HALO], chunk_rows(2 * pair + h), below[h * HALO:(h + 1) * HALO]], axis=0
            )
            for h in (0, 1)
        ]

    def each_wide(which, source, chunk_rows, put):
        for pair in range(CHUNKS // 2):
            for h, value in enumerate(widened(which, source, chunk_rows, pair)):
                put(2 * pair + h, value)

    def landed(which, source):
        return lambda j: strip_land[which, source, j].astype(F32)

    lane = lax.broadcasted_iota(jnp.int32, (WIDE, LANES), 1)
    leftmost, rightmost = lane == 0, lane == LANES - 1

    def spread(before, now, now_left, after_left):
        now_right = pltpu.roll(now, 1, 1)
        total = (
            jnp.where(leftmost, before, now_right) + jnp.where(rightmost, after_left, now_left)
            + pltpu.roll(now, 1, 0) + pltpu.roll(now, WIDE - 1, 0) - 4.0 * now
        )
        return total, now_right

    def run_steps(diff, adjoint):
        nothing = jnp.zeros((WIDE, LANES), F32)

        @pl.loop(0, STEPS)
        def _(step):
            field = work[1]
            before, now = nothing, diff[1] * field if adjoint else field
            now_left = pltpu.roll(now, LANES - 1, 1)
            for j in range(1, CHUNKS + 1):
                later = after = after_left = nothing
                if j < CHUNKS:
                    later = work[j + 1]
                    after = diff[j + 1] * later if adjoint else later
                    after_left = pltpu.roll(after, LANES - 1, 1)
                total, now_right = spread(before, now, now_left, after_left)
                work[j] = field + total if adjoint else now + diff[j] * total
                before, now, now_left, field = now_right, after, after_left, later

    def put_work(j, value):
        work[j + 1] = value

    row = lax.broadcasted_iota(jnp.int32, (WIDE, LANES), 0)
    inside = ~((row < HALO) & top) & ~((row >= HALO + ROWS) & bottom)

    low_of = (4, MULT, MULT + 1)

    def chip_at(to):
        return (sub, to * 2 + core)

    def apart(low, high):
        return lax.rem(high - low + 16, 16)

    def there_copy(phase, to):
        at = apart(chip, to)
        return remote(strip_mine.at[low_of[phase], to], low_land.at[phase, chip, core],
                      there_send.at[phase, at], there_recv.at[phase, at], chip_at(to))

    def there_own(phase):
        low_land[phase, chip, core] = strip_mine[low_of[phase], chip]

    def core_copy(phase, row):
        mine = low_land.at[phase, pl.ds(4 * row, 4), core]
        at = lax.rem(row - y + 4, 4)
        return remote(mine, mine, core_send.at[phase, at], core_recv.at[phase, at], peer)

    def back_copy(phase, to):
        at = apart(chip, to)
        return remote(half_mine.at[phase, to], half_land.at[phase, chip],
                      back_send.at[phase, at], back_recv.at[phase, at], chip_at(to))

    def from_row(make, recv, phase, d_row):
        row = lax.rem(y + d_row, 4)
        for d_z in range(1 if d_row == 0 else 0, 4):
            source = row * 4 + lax.rem(z + d_z, 4)
            copy = make(phase, source)
            at = apart(source, chip)
            remote(copy.src_ref, copy.dst_ref, recv.at[phase, at], recv.at[phase, at], peer).wait_recv()
        return row

    ORDER = (0, 1, 3, 2)

    def north_product(phase):
        rows = []

        def arrive(d_row):
            row = from_row(there_copy, there_recv, phase, d_row)
            core_copy(phase, row).start()
            rows.append(row)

        def columns(row):
            return low_land[phase, pl.ds(4 * row, 4)].reshape(4 * 2 * ROWS, LANES)

        arrive(ORDER[0])
        for number in range(4):
            if number < 3:
                arrive(ORDER[number + 1])
            row = rows[number]
            core_copy(phase, row).wait_recv()
            depth = pl.ds(pl.multiple_of(512 * row, 512), 512)
            if number < 3:
                product = jnp.dot(
                    north_all[:, :, depth].reshape(1024, 512), columns(row), preferred_element_type=F32)
                north_sum[...] = product if number == 0 else north_sum[...] + product
                continue
            for d_row in (2, 1, 3, 0):
                to_row = lax.rem(y + d_row, 4)
                part = pl.ds(pl.multiple_of(256 * to_row, 256), 256)
                product = jnp.dot(
                    north_all[pl.ds(4 * to_row, 4), :, depth].reshape(256, 512), columns(row),
                    preferred_element_type=F32)
                half = (north_sum[part, :] + product).astype(BF16).reshape(4, ROWS, LANES)
                half_mine[phase, pl.ds(4 * to_row, 4)] = half
                for d_z in range(1 if d_row == 0 else 0, 4):
                    back_copy(phase, to_row * 4 + lax.rem(z + d_z, 4)).start()
        half_land[phase, chip] = half_mine[phase, chip]

    def east_product(phase, finish):
        for number, d_row in enumerate(ORDER):
            row = from_row(back_copy, back_recv, phase, d_row)
            left = jnp.concatenate([half_land[phase, 4 * row + c] for c in range(4)], axis=1)
            depth = pl.ds(pl.multiple_of(512 * row, 512), 512)
            if number < 3:
                product = jnp.dot(left, east_all[depth, :], preferred_element_type=F32)
                east_sum[...] = product if number == 0 else east_sum[...] + product
                continue
            for d_pair in range(8):
                pair = lax.rem(lax.div(chip, 2) + d_pair, 8)
                part = pl.ds(pl.multiple_of(256 * pair, 256), 256)
                product = east_sum[:, part] + jnp.dot(left, east_all[depth, part], preferred_element_type=F32)
                for h in (0, 1):
                    finish(2 * pair + h, product[:, LANES * h:LANES * (h + 1)], d_pair == 0)

    loaded(mult, load_sem.at[0])
    for j in range(CHUNKS):
        strip_mine[4, j] = mult[j].astype(BF16)
    for offset in range(1, 16):
        there_copy(0, plane(offset)[0]).start()
    there_own(0)
    loaded(force, load_sem.at[2])
    pack(DIFF, force)
    swap_start(DIFF)
    loaded(incr_own, load_sem.at[1])
    pack(INCR, incr_own)
    swap_start(INCR)
    gather_first_ring()
    gather_own_second()
    relay_across(DIFF)
    relay_across(INCR)
    gather_far()
    swap_wait_number(DIFF, FROM_SAME)

    def put_own(j, value):
        diff_own[j + 1] = value

    each_wide(DIFF, 1, lambda j: force[j], put_own)
    load(forcing.at[0], force, load_sem.at[2])
    relay_to_hub(DIFF)
    relay_to_hub(INCR)
    own_north.wait()
    gather_rest()
    north_product(0)
    swap_wait_number(DIFF, FROM_BEFORE)
    relay_end(DIFF, 4)

    def put_prev(j, value):
        diff_prev[j + 1] = value

    each_wide(DIFF, 0, landed(DIFF, 0), put_prev)
    swap_wait_number(INCR, FROM_BEFORE)
    relay_end(INCR, 4)

    def put_incr(j, value):
        incr_prev[j] = value
        work[j + 1] = value

    each_wide(INCR, 0, landed(INCR, 0), put_incr)
    run_steps(diff_prev, False)
    loaded(force, load_sem.at[2])
    for j in range(CHUNKS):
        model[j] = force[j] - incr_own[j] + jnp.where(first, 0.0, work[j + 1, HALO:HALO + ROWS])
    own_east.wait()

    def update(phase):
        def finish(j, product, own):
            value = mult[j] + 0.5 * (model[j] - product)
            mult[j] = value
            rounded = value.astype(BF16)
            strip_mine[low_of[phase + 1], j] = rounded
            if not own:
                there_copy(phase + 1, j).start()
            else:
                @pl.when(j != chip)
                def _():
                    there_copy(phase + 1, j).start()
        return finish

    east_product(0, update(0))

    for phase in range(1, PHASES):
        which = MULT - 1 + phase
        final = phase == PHASES - 1
        there_own(phase)
        pack(which, mult)
        swap_start(which)
        swap_wait_number(which, FROM_SAME)
        each_wide(which, 1, lambda j: mult[j], put_work)
        relay_across(which)
        run_steps(diff_prev, True)
        for j in range(CHUNKS):
            incr_prev[j] = incr_prev[j] - 0.5 * work[j + 1]
        north_product(phase)
        relay_to_hub(which)
        swap_wait_number(which, FROM_BEFORE)
        relay_end(which, 4)

        def put_before(j, value):
            value = jnp.where(inside, incr_prev[j] + 0.5 * value, 0.0)
            incr_prev[j] = value
            work[j + 1] = value

        each_wide(which, 0, landed(which, 0), put_before)
        run_steps(diff_prev, False)
        for j in range(CHUNKS):
            model[j] = force[j] + jnp.where(first, 0.0, work[j + 1, HALO:HALO + ROWS])
        swap_wait_number(which, FROM_AFTER)
        relay_end(which, 3)
        each_wide(which, 2, landed(which, 1), put_work)
        run_steps(diff_own, True)

        def stored(source, target, j, sem):
            columns = pl.ds(pl.multiple_of(LANES * j, LANES), LANES)
            pltpu.make_async_copy(source, target.at[0, :, columns], sem).start()

        for j in range(CHUNKS):
            grad = mult[j] - jnp.where(last, 0.0, work[j + 1, HALO:HALO + ROWS])
            incr = incr_own[j] + 0.5 * grad
            incr_own[j] = incr
            model[j] = model[j] - incr
            if final:
                force[j] = grad
                stored(force.at[j], grad_out, j, out_sem.at[0])

        if not final:
            east_product(phase, update(phase))
        else:
            def finish(j, product, own):
                mult[j] = model[j] - product
                stored(mult.at[j], mult_out, j, out_sem.at[1])

            east_product(phase, finish)

    for copy in gather_sends:
        copy.wait_send()
    for phase in range(PHASES):
        for offset in range(1, 16):
            there_copy(phase, plane(offset)[0]).wait_send()
            back_copy(phase, plane(offset)[0]).wait_send()
        for row in range(4):
            core_copy(phase, row).wait_send()
    for which in (DIFF, INCR, MULT, MULT + 1):
        for copy, sent, _ in swap_copies(which):
            pl.when(sent)(copy.wait_send)
        relay_sent(which)
    pltpu.make_async_copy(model, model, out_sem.at[0]).wait()
    pltpu.make_async_copy(model, model, out_sem.at[1]).wait()


def local(forcing, mult_start, incr_start, diffusivity, north_corr, east_corr):
    any_space = pl.BlockSpec(memory_space=pl.ANY)
    dma = pltpu.SemaphoreType.DMA
    strip = (CHUNKS, ROWS, LANES)
    wide = (CHUNKS, WIDE, LANES)
    padded = (CHUNKS + 2, WIDE, LANES)
    pieces = len(GATHER_PARTS)
    out = jax.ShapeDtypeStruct((1, ROWS, 2048), F32)
    return pl.pallas_call(
        kernel,
        out_shape=(out, out),
        in_specs=[any_space] * 6,
        out_specs=(any_space, any_space),
        scratch_shapes=[
            pltpu.VMEM((16, ROWS, 2048), BF16),
            pltpu.VMEM((2048, 2048), BF16),
            pltpu.VMEM((PHASES, 16, 2, ROWS, LANES), BF16),
            pltpu.VMEM((PHASES,) + strip, BF16),
            pltpu.VMEM((PHASES,) + strip, BF16),
            pltpu.VMEM((4, 2) + strip, BF16),
            pltpu.VMEM((4, 3, 2, CHUNKS // 2, 2 * HALO, LANES), BF16),
            pltpu.VMEM((5,) + strip, BF16),
            pltpu.VMEM((4, 2, CHUNKS // 2, 2 * HALO, LANES), BF16),
            pltpu.VMEM(padded, F32),
            pltpu.VMEM(padded, F32),
            pltpu.VMEM(padded, F32),
            pltpu.VMEM(wide, F32),
            pltpu.VMEM(strip, F32),
            pltpu.VMEM(strip, F32),
            pltpu.VMEM(strip, F32),
            pltpu.VMEM(strip, F32),
            pltpu.VMEM((1024, LANES), F32),
            pltpu.VMEM((ROWS, 2048), F32),
            pltpu.VMEM((4, 4, ROWS, LANES), BF16),
            pltpu.VMEM((4, 4, ROWS, LANES), BF16),
            dma((5,)),
            dma((pieces * 20,)),
            dma((pieces * 32,)),
            dma((PHASES, 16)),
            dma((PHASES, 16)),
            dma((PHASES, 4)),
            dma((PHASES, 4)),
            dma((PHASES, 16)),
            dma((PHASES, 16)),
            dma((4, 8)),
            dma((4, 8)),
            dma((4, 6)),
            dma((4, 6)),
            dma((2,)),
        ],
        compiler_params=pltpu.CompilerParams(
            collective_id=0, has_side_effects=True, vmem_limit_bytes=48 * 2**20
        ),
    )(forcing, mult_start, incr_start, diffusivity, north_corr, east_corr)


def solution(mesh):
    rows = P("sub", "strip", None)
    return jax.shard_map(
        local,
        mesh=mesh,
        in_specs=(rows, rows, rows, rows, P("strip", None), P()),
        out_specs=(rows, rows),
        check_vma=False,
    )
```

```python
import functools

import jax
import jax.numpy as jnp
from jax import lax
from jax.experimental import pallas as pl
from jax.experimental.pallas import tpu as pltpu
from jax.sharding import PartitionSpec as P

STEPS = 4
ITERS = 2
PHASES = ITERS + 1
MESH = pl.DeviceIdType.MESH
F32, BF16 = jnp.float32, jnp.bfloat16

ROWS, WIDE, CHUNKS, LANES = 64, 80, 16, 128
HALO = 8
GATHER_PARTS = ((0, 768, "zy"), (768, 512, "yz"), (1280, 768, "yzx"))

DIFF, INCR, MULT = 0, 1, 2


def kernel(forcing, mult_in, incr_in, diff_in, north, east, mult_out, grad_out,
           north_all, east_all, low_land, half_land, half_mine, strip_land, rim_land, strip_mine, rim_mine,
           work, diff_prev, diff_own, incr_prev, incr_own, mult, force, model, grad_kept, north_sum, east_sum, relay_out, relay_in,
           load_sem, gather_send, gather_recv, shared_send, shared_recv, there_send, there_recv, core_send, core_recv, back_send, back_recv,
           swap_send, swap_recv, relay_send, relay_recv, out_sem):
    sub, strip = lax.axis_index("sub"), lax.axis_index("strip")
    x, z_hi = lax.rem(sub, 4), lax.div(sub, 4)
    y, z, core = lax.div(strip, 8), lax.rem(lax.div(strip, 2), 4), lax.rem(strip, 2)
    chip, z_all = y * 4 + z, z_hi * 4 + z

    def device(x_at, y_at, z_at):
        return (lax.div(z_at, 4) * 4 + x_at, y_at * 8 + lax.rem(z_at, 4) * 2 + core)

    def along(dim, step):
        if dim == "y":
            return device(x, lax.rem(y + step + 4, 4), z_all)
        return device(x, y, lax.rem(z_all + step + 8, 8))

    peer = (sub, strip + 1 - 2 * core)

    def plane(offset):
        to = lax.rem(chip + offset, 16)
        return to, (sub, to * 2 + core)

    def remote(src, dst, send, recv, to):
        return pltpu.make_async_remote_copy(
            src_ref=src, dst_ref=dst, send_sem=send, recv_sem=recv, device_id=to, device_id_type=MESH
        )

    first, last = sub == 0, sub == 7
    top, bottom = strip == 0, strip == 31
    hub = jnp.where(z_hi == 0, 3, 4)
    is_hub = sub == hub
    across = (lax.rem(sub + 4, 8), strip)

    rim_land[...] = jnp.zeros_like(rim_land)
    for ref in (work, diff_prev, diff_own):
        ref[0] = jnp.zeros((WIDE, LANES), F32)
        ref[CHUNKS + 1] = jnp.zeros((WIDE, LANES), F32)

    barrier = pltpu.get_barrier_semaphore()

    def greet(to):
        pl.semaphore_signal(barrier, inc=1, device_id=to, device_id_type=MESH)

    for offset in range(1, 16):
        greet(plane(offset)[1])
    greet(peer)
    greet(across)
    for step in (-2, -1, 1, 2):
        greet(along("z", step))
    for step in (-1, 1):
        greet(device(lax.rem(x + step + 4, 4), y, z_all))
    near = [
        (-1, 0, ~first), (1, 0, ~last),
        (-1, -1, ~first & ~top), (-1, 1, ~first & ~bottom),
        (1, -1, ~last & ~top), (1, 1, ~last & ~bottom),
        (0, -1, ~top), (0, 1, ~bottom),
    ]
    for d_sub, d_strip, there in near:
        @pl.when(there)
        def _(d_sub=d_sub, d_strip=d_strip):
            greet((sub + d_sub, strip + d_strip))
    for part in range(4):
        @pl.when(is_hub & (x != part))
        def _(part=part):
            greet((z_hi * 4 + part, strip))

    @pl.when(~is_hub)
    def _():
        greet((hub, strip))

    expected = 23 + jnp.where(is_hub, 3, 1)
    for _, _, there in near:
        expected = expected + there.astype(jnp.int32)
    def load(source, target, sem):
        for j in range(CHUNKS):
            pltpu.make_async_copy(source.at[:, pl.ds(LANES * j, LANES)], target.at[j], sem).start()

    def loaded(target, sem):
        pltpu.make_async_copy(target, target, sem).wait()

    load(mult_in.at[0], mult, load_sem.at[0])
    load(incr_in.at[0], incr_own, load_sem.at[1])
    load(diff_in.at[0], force, load_sem.at[2])
    shared = GATHER_PARTS[2][0]
    own_rows = pl.ds(pl.multiple_of(16 * x, 16), 16)
    own_north = [
        pltpu.make_async_copy(north.at[:, pl.ds(0, shared)], north_all.at[chip, :, pl.ds(0, shared)], load_sem.at[3]),
        pltpu.make_async_copy(
            north.at[own_rows, pl.ds(shared, 2048 - shared)],
            north_all.at[chip, own_rows, pl.ds(shared, 2048 - shared)], load_sem.at[5]),
    ]
    for copy in own_north:
        copy.start()
    own_east = pltpu.make_async_copy(east, east_all, load_sem.at[4])
    own_east.start()
    pl.semaphore_wait(barrier, expected)

    gather_sends = []

    def gather_copy(part, piece, half, source, to, recv_at, sends):
        start, size, order = GATHER_PARTS[part]
        if half is not None:
            width = size // 2 // LANES * LANES
            start, size = (start, width) if half == 0 else (start + width, size - width)
        columns = pl.ds(start, size)
        rows = pl.ds(pl.multiple_of(16 * x, 16), 16) if "x" in order else pl.ds(0, ROWS)
        source = source.at[rows, columns] if source is north else source.at[piece, rows, columns]
        return remote(source, north_all.at[piece, rows, columns], gather_send.at[sends], gather_recv.at[recv_at], to)

    def slot(part, rel_a, rel_b, half):
        return ((part * 4 + rel_a) * 4 + rel_b) * 2 + (half or 0)

    def piece_of(part, rel_a, rel_b):
        rel_z, rel_y = (rel_a, rel_b) if GATHER_PARTS[part][2][0] == "z" else (rel_b, rel_a)
        return lax.rem(y + rel_y, 4) * 4 + lax.rem(z + rel_z, 4)

    def gather_put(part, rel_a, rel_b, ring, step, half=None):
        to_a, to_b = ((rel_a - step) % 4, rel_b) if ring == 0 else (rel_a, (rel_b - step) % 4)
        copy = gather_copy(
            part, piece_of(part, rel_a, rel_b), half, north if (rel_a, rel_b) == (0, 0) else north_all,
            along(GATHER_PARTS[part][2][ring], step), slot(part, to_a, to_b, half), len(gather_sends),
        )
        copy.start()
        gather_sends.append(copy)

    def gather_wait(part, rel_a, rel_b, half=None):
        gather_copy(part, piece_of(part, rel_a, rel_b), half, north_all, peer, slot(part, rel_a, rel_b, half), 0).wait_recv()

    parts = range(len(GATHER_PARTS))

    def gather_start():
        for part in parts:
            gather_put(part, 0, 0, 0, 1)
            gather_put(part, 0, 0, 0, -1)
        for part in parts:
            gather_put(part, 0, 0, 1, 1)
            gather_put(part, 0, 0, 1, -1)
            gather_put(part, 0, 0, 0, 2)

    def gather_first(rel):
        for part in parts:
            gather_wait(part, rel, 0)
            gather_put(part, rel, 0, 1, 1)
            gather_put(part, rel, 0, 1, -1)

    def gather_second(rel_a):
        for part in parts:
            for rel, step in ((3, 1), (1, -1)):
                gather_wait(part, rel_a, rel)
                gather_put(part, rel_a, rel, 1, step, half=0 if step == 1 else 1)

    def gather_far(rel_a):
        for part in parts:
            gather_wait(part, rel_a, 2, 0)
            gather_wait(part, rel_a, 2, 1)

    def shared_ref(rel_a, far, half):
        start, size, _ = GATHER_PARTS[2]
        if half is not None:
            start, size = start + half * (size // 2), size // 2
        at = lax.rem(y + rel_a, 4)
        rows = pl.ds(pl.multiple_of(16 * lax.rem(x + far, 4), 16), 16)
        return north_all.at[pl.ds(4 * at, 4), rows, pl.ds(start, size)]

    def shared_put(rel_a, far, step, half=None):
        ref = shared_ref(rel_a, far, half)
        at = (rel_a * 4 + (far - step) % 4) * 2 + (half or 0)
        copy = remote(ref, ref, shared_send.at[len(shared_sends)], shared_recv.at[at],
                      device(lax.rem(x + step + 4, 4), y, z_all))
        copy.start()
        shared_sends.append(copy)

    def shared_wait(rel_a, far, half=None):
        ref = shared_ref(rel_a, far, half)
        at = (rel_a * 4 + far) * 2 + (half or 0)
        remote(ref, ref, shared_recv.at[at], shared_recv.at[at], peer).wait_recv()

    shared_sends = []

    def shared_start(rel_a):
        for _ in parts[:1]:
            shared_put(rel_a, 0, 1)
            shared_put(rel_a, 0, -1)

    def shared_on(rel_a):
        for _ in parts[:1]:
            shared_wait(rel_a, 3)
            shared_put(rel_a, 3, 1, half=0)
            shared_wait(rel_a, 1)
            shared_put(rel_a, 1, -1, half=1)

    def shared_end(rel_a):
        for _ in parts[:1]:
            shared_wait(rel_a, 2, 0)
            shared_wait(rel_a, 2, 1)

    gather_start()

    def swap_copies(which):
        copies = []
        for at, d_sub in ((0, 1), (1, -1)):
            if which < MULT and d_sub == -1:
                continue
            sent = ~last & (sub != 3) if d_sub == 1 else ~first & (sub != 4)
            heard = ~first & (sub != 4) if d_sub == 1 else ~last & (sub != 3)
            copies.append((remote(
                strip_mine.at[which], strip_land.at[which, at], swap_send.at[which, at],
                swap_recv.at[which, at], (sub + d_sub, strip)), sent, heard))
        for at, d_sub in ((0, 1), (1, 0), (2, -1)):
            if (which == INCR and d_sub == 0) or (which < MULT and d_sub == -1):
                continue
            sub_sent = {1: ~last, 0: first | ~first, -1: ~first}[d_sub]
            sub_heard = {1: ~first, 0: first | ~first, -1: ~last}[d_sub]
            for edge, d_strip in ((0, -1), (1, 1)):
                sent = sub_sent & (~top if d_strip == -1 else ~bottom)
                heard = sub_heard & (~bottom if d_strip == -1 else ~top)
                number = 2 + 2 * at + edge
                copies.append((remote(
                    rim_mine.at[which, edge], rim_land.at[which, at, 1 - edge], swap_send.at[which, number],
                    swap_recv.at[which, number], (sub + d_sub, strip + d_strip)), sent, heard))
        return copies

    def swap_start(which):
        relay_from_hub(which)
        for copy, sent, _ in swap_copies(which):
            pl.when(sent)(copy.start)

    def swap_wait_number(which, numbers):
        copies = swap_copies(which)
        order = ([0, 1] if which >= MULT else [0]) + [
            2 + 2 * at + edge
            for at, d_sub in ((0, 1), (1, 0), (2, -1))
            if not ((which == INCR and d_sub == 0) or (which < MULT and d_sub == -1))
            for edge in (0, 1)
        ]
        for number, (copy, _, heard) in zip(order, copies, strict=True):
            if number in numbers:
                pl.when(heard)(copy.wait_recv)

    def relay_copies(which):
        up_only = which < MULT
        gives = z_hi == 0 if up_only else z_hi >= 0
        takes = z_hi == 1 if up_only else z_hi >= 0
        land = 0 if up_only else jnp.where(z_hi == 0, 1, 0)
        far_land = 0 if up_only else 1 - land
        quarter = lambda ref, part: ref.at[pl.ds(4 * part, 4)]
        send, recv = relay_send.at[which], relay_recv.at[which]
        outward = [
            (remote(quarter(strip_mine.at[which], part), relay_out.at[which], send.at[part], recv.at[0],
                    (z_hi * 4 + part, strip)), gives & is_hub & (x != part))
            for part in range(4)
        ]
        mine, kept = quarter(strip_mine.at[which], x), relay_out.at[which]
        there, there_kept = quarter(strip_land.at[which, far_land], x), relay_in.at[which]
        far_hub = across[0] == 7 - hub
        over = [
            (remote(mine, there_kept, send.at[4], recv.at[1], across), gives & is_hub),
            (remote(kept, there, send.at[4], recv.at[1], across), gives & ~is_hub & far_hub),
            (remote(kept, there_kept, send.at[4], recv.at[1], across), gives & ~is_hub & ~far_hub),
        ]
        inward = (remote(relay_in.at[which], quarter(strip_land.at[which, land], x), send.at[5], recv.at[2 + x], (hub, strip)),
                  takes & ~is_hub)
        waits = {
            "out": (outward[0][0], gives & ~is_hub),
            "over": (over[0][0], takes),
            "in": [
                (remote(relay_in.at[which], quarter(strip_land.at[which, land], part), send.at[5], recv.at[2 + part], (hub, strip)),
                 takes & is_hub & (x != part))
                for part in range(4)
            ],
        }
        return outward, over, inward, waits

    def relay_from_hub(which):
        outward, over, _, _ = relay_copies(which)
        pl.when(over[0][1])(over[0][0].start)
        for copy, sent in outward:
            pl.when(sent)(copy.start)

    def relay_across(which):
        _, over, _, waits = relay_copies(which)
        copy, heard = waits["out"]
        pl.when(heard)(copy.wait_recv)
        for copy, sent in over[1:]:
            pl.when(sent)(copy.start)

    def relay_to_hub(which):
        _, _, (copy, sent), waits = relay_copies(which)
        arrived, heard = waits["over"]
        pl.when(heard)(arrived.wait_recv)
        pl.when(sent)(copy.start)

    def relay_end(which, hub_sub):
        for copy, heard in relay_copies(which)[3]["in"]:
            pl.when(heard & (sub == hub_sub))(copy.wait_recv)

    def relay_sent(which):
        outward, over, (copy, sent), _ = relay_copies(which)
        for one, was in outward:
            pl.when(was)(one.wait_send)
        gives = over[0][1] | over[1][1] | over[2][1]
        pl.when(gives)(over[0][0].wait_send)
        pl.when(sent)(copy.wait_send)

    FROM_BEFORE, FROM_SAME, FROM_AFTER = (0, 2, 3), (4, 5), (1, 6, 7)

    def pack(which, field):
        for pair in range(CHUNKS // 2):
            left, right = field[2 * pair], field[2 * pair + 1]
            if which < MULT:
                strip_mine[which, 2 * pair] = left.astype(BF16)
                strip_mine[which, 2 * pair + 1] = right.astype(BF16)
            rim_mine[which, 0, pair] = jnp.concatenate([left[:HALO], right[:HALO]], axis=0).astype(BF16)
            rim_mine[which, 1, pair] = jnp.concatenate([left[-HALO:], right[-HALO:]], axis=0).astype(BF16)

    def widened(which, source, chunk_rows, pair):
        above = rim_land[which, source, 0, pair].astype(F32)
        below = rim_land[which, source, 1, pair].astype(F32)
        return [
            jnp.concatenate(
                [above[h * HALO:(h + 1) * HALO], chunk_rows(2 * pair + h), below[h * HALO:(h + 1) * HALO]], axis=0
            )
            for h in (0, 1)
        ]

    def each_wide(which, source, chunk_rows, put):
        for pair in range(CHUNKS // 2):
            for h, value in enumerate(widened(which, source, chunk_rows, pair)):
                put(2 * pair + h, value)

    def landed(which, source):
        return lambda j: strip_land[which, source, j].astype(F32)

    lane = lax.broadcasted_iota(jnp.int32, (WIDE, LANES), 1)
    leftmost, rightmost = lane == 0, lane == LANES - 1

    def spread(before, now, now_left, after_left):
        now_right = pltpu.roll(now, 1, 1)
        total = (
            jnp.where(leftmost, before, now_right) + jnp.where(rightmost, after_left, now_left)
            + pltpu.roll(now, 1, 0) + pltpu.roll(now, WIDE - 1, 0) - 4.0 * now
        )
        return total, now_right

    def run_steps(diff, adjoint):
        nothing = jnp.zeros((WIDE, LANES), F32)

        @pl.loop(0, STEPS)
        def _(step):
            field = work[1]
            before, now = nothing, diff[1] * field if adjoint else field
            now_left = pltpu.roll(now, LANES - 1, 1)
            for j in range(1, CHUNKS + 1):
                later = after = after_left = nothing
                if j < CHUNKS:
                    later = work[j + 1]
                    after = diff[j + 1] * later if adjoint else later
                    after_left = pltpu.roll(after, LANES - 1, 1)
                total, now_right = spread(before, now, now_left, after_left)
                work[j] = field + total if adjoint else now + diff[j] * total
                before, now, now_left, field = now_right, after, after_left, later

    def put_work(j, value):
        work[j + 1] = value

    row = lax.broadcasted_iota(jnp.int32, (WIDE, LANES), 0)
    inside = ~((row < HALO) & top) & ~((row >= HALO + ROWS) & bottom)

    low_of = (4, MULT, MULT + 1)

    def chip_at(to):
        return (sub, to * 2 + core)

    def apart(low, high):
        return lax.rem(high - low + 16, 16)

    def there_copy(phase, to):
        at = apart(chip, to)
        return remote(strip_mine.at[low_of[phase], to], low_land.at[phase, chip, core],
                      there_send.at[phase, at], there_recv.at[phase, at], chip_at(to))

    def there_own(phase):
        low_land[phase, chip, core] = strip_mine[low_of[phase], chip]

    def core_copy(phase, row):
        mine = low_land.at[phase, pl.ds(4 * row, 4), core]
        at = lax.rem(row - y + 4, 4)
        return remote(mine, mine, core_send.at[phase, at], core_recv.at[phase, at], peer)

    def back_copy(phase, to):
        at = apart(chip, to)
        return remote(half_mine.at[phase, to], half_land.at[phase, chip],
                      back_send.at[phase, at], back_recv.at[phase, at], chip_at(to))

    def from_row(make, recv, phase, d_row):
        row = lax.rem(y + d_row, 4)
        for d_z in range(1 if d_row == 0 else 0, 4):
            source = row * 4 + lax.rem(z + d_z, 4)
            copy = make(phase, source)
            at = apart(source, chip)
            remote(copy.src_ref, copy.dst_ref, recv.at[phase, at], recv.at[phase, at], peer).wait_recv()
        return row

    ORDER = (0, 1, 3, 2)

    def north_product(phase):
        rows = []

        def arrive(d_row):
            row = from_row(there_copy, there_recv, phase, d_row)
            core_copy(phase, row).start()
            rows.append(row)

        def columns(row):
            return low_land[phase, pl.ds(4 * row, 4)].reshape(4 * 2 * ROWS, LANES)

        arrive(ORDER[0])
        for number in range(4):
            if number < 3:
                arrive(ORDER[number + 1])
            row = rows[number]
            core_copy(phase, row).wait_recv()
            depth = pl.ds(pl.multiple_of(512 * row, 512), 512)
            if number < 3:
                product = jnp.dot(
                    north_all[:, :, depth].reshape(1024, 512), columns(row), preferred_element_type=F32)
                north_sum[...] = product if number == 0 else north_sum[...] + product
                continue
            for d_row in (2, 1, 3, 0):
                to_row = lax.rem(y + d_row, 4)
                part = pl.ds(pl.multiple_of(256 * to_row, 256), 256)
                product = jnp.dot(
                    north_all[pl.ds(4 * to_row, 4), :, depth].reshape(256, 512), columns(row),
                    preferred_element_type=F32)
                half = (north_sum[part, :] + product).astype(BF16).reshape(4, ROWS, LANES)
                half_mine[phase, pl.ds(4 * to_row, 4)] = half
                for d_z in range(1 if d_row == 0 else 0, 4):
                    back_copy(phase, to_row * 4 + lax.rem(z + d_z, 4)).start()
        half_land[phase, chip] = half_mine[phase, chip]

    def east_product(phase, finish):
        for number, d_row in enumerate(ORDER):
            row = from_row(back_copy, back_recv, phase, d_row)
            left = jnp.concatenate([half_land[phase, 4 * row + c] for c in range(4)], axis=1)
            depth = pl.ds(pl.multiple_of(512 * row, 512), 512)
            if number < 3:
                product = jnp.dot(left, east_all[depth, :], preferred_element_type=F32)
                east_sum[...] = product if number == 0 else east_sum[...] + product
                continue
            for d_pair in range(8):
                pair = lax.rem(lax.div(chip, 2) + d_pair, 8)
                part = pl.ds(pl.multiple_of(256 * pair, 256), 256)
                product = east_sum[:, part] + jnp.dot(left, east_all[depth, part], preferred_element_type=F32)
                for h in (0, 1):
                    finish(2 * pair + h, product[:, LANES * h:LANES * (h + 1)], d_pair == 0)

    loaded(mult, load_sem.at[0])
    for j in range(CHUNKS):
        strip_mine[4, j] = mult[j].astype(BF16)
    for offset in range(1, 16):
        there_copy(0, plane(offset)[0]).start()
    there_own(0)
    loaded(force, load_sem.at[2])
    pack(DIFF, force)
    swap_start(DIFF)
    loaded(incr_own, load_sem.at[1])
    pack(INCR, incr_own)
    swap_start(INCR)
    gather_first(3)
    gather_first(1)
    for copy in own_north:
        copy.wait()
    gather_second(0)
    gather_first(2)
    relay_across(DIFF)
    relay_across(INCR)
    gather_far(0)
    shared_start(0)
    swap_wait_number(DIFF, FROM_SAME)

    def put_own(j, value):
        diff_own[j + 1] = value

    each_wide(DIFF, 1, lambda j: force[j], put_own)
    load(forcing.at[0], force, load_sem.at[2])
    relay_to_hub(DIFF)
    relay_to_hub(INCR)
    for rel_a in (3, 1):
        gather_second(rel_a)
        gather_far(rel_a)
        shared_start(rel_a)
    shared_on(0)
    gather_second(2)
    gather_far(2)
    shared_start(2)
    for rel_a in (3, 1, 2):
        shared_on(rel_a)
    for rel_a in (0, 3, 1, 2):
        shared_end(rel_a)
    north_product(0)
    swap_wait_number(DIFF, FROM_BEFORE)
    relay_end(DIFF, 4)

    def put_prev(j, value):
        diff_prev[j + 1] = value

    each_wide(DIFF, 0, landed(DIFF, 0), put_prev)
    swap_wait_number(INCR, FROM_BEFORE)
    relay_end(INCR, 4)

    def put_incr(j, value):
        incr_prev[j] = value
        work[j + 1] = value

    each_wide(INCR, 0, landed(INCR, 0), put_incr)
    run_steps(diff_prev, False)
    loaded(force, load_sem.at[2])
    for j in range(CHUNKS):
        model[j] = force[j] - incr_own[j] + jnp.where(first, 0.0, work[j + 1, HALO:HALO + ROWS])
    own_east.wait()

    def update(phase):
        def finish(j, product, own):
            value = mult[j] + 0.5 * (model[j] - product)
            mult[j] = value
            rounded = value.astype(BF16)
            strip_mine[low_of[phase + 1], j] = rounded
            if not own:
                there_copy(phase + 1, j).start()
            else:
                @pl.when(j != chip)
                def _():
                    there_copy(phase + 1, j).start()
        return finish

    east_product(0, update(0))

    for phase in range(1, PHASES):
        which = MULT - 1 + phase
        final = phase == PHASES - 1
        there_own(phase)
        pack(which, mult)
        swap_start(which)
        swap_wait_number(which, FROM_SAME)
        each_wide(which, 1, lambda j: mult[j], put_work)
        relay_across(which)
        run_steps(diff_prev, True)
        for j in range(CHUNKS):
            incr_prev[j] = incr_prev[j] - 0.5 * work[j + 1]
        north_product(phase)
        relay_to_hub(which)
        def stored(source, target, j, sem):
            columns = pl.ds(pl.multiple_of(LANES * j, LANES), LANES)
            pltpu.make_async_copy(source, target.at[0, :, columns], sem).start()

        def own_increments():
            swap_wait_number(which, FROM_AFTER)
            relay_end(which, 3)
            each_wide(which, 2, landed(which, 1), put_work)
            run_steps(diff_own, True)
            for j in range(CHUNKS):
                grad = mult[j] - jnp.where(last, 0.0, work[j + 1, HALO:HALO + ROWS])
                incr_own[j] = incr_own[j] + 0.5 * grad
                if final:
                    grad_kept[j] = grad
                    stored(grad_kept.at[j], grad_out, j, out_sem.at[0])

        pl.when(sub != 3)(own_increments)
        swap_wait_number(which, FROM_BEFORE)
        relay_end(which, 4)

        def put_before(j, value):
            value = jnp.where(inside, incr_prev[j] + 0.5 * value, 0.0)
            incr_prev[j] = value
            work[j + 1] = value

        each_wide(which, 0, landed(which, 0), put_before)
        run_steps(diff_prev, False)
        for j in range(CHUNKS):
            model[j] = force[j] + jnp.where(first, 0.0, work[j + 1, HALO:HALO + ROWS])
        pl.when(sub == 3)(own_increments)
        for j in range(CHUNKS):
            model[j] = model[j] - incr_own[j]
        if not final:
            east_product(phase, update(phase))
        else:
            def finish(j, product, own):
                mult[j] = model[j] - product
                stored(mult.at[j], mult_out, j, out_sem.at[1])

            east_product(phase, finish)

    for copy in gather_sends + shared_sends:
        copy.wait_send()
    for phase in range(PHASES):
        for offset in range(1, 16):
            there_copy(phase, plane(offset)[0]).wait_send()
            back_copy(phase, plane(offset)[0]).wait_send()
        for row in range(4):
            core_copy(phase, row).wait_send()
    for which in (DIFF, INCR, MULT, MULT + 1):
        for copy, sent, _ in swap_copies(which):
            pl.when(sent)(copy.wait_send)
        relay_sent(which)
    pltpu.make_async_copy(model, model, out_sem.at[0]).wait()
    pltpu.make_async_copy(model, model, out_sem.at[1]).wait()


def local(forcing, mult_start, incr_start, diffusivity, north_corr, east_corr):
    any_space = pl.BlockSpec(memory_space=pltpu.HBM)
    dma = pltpu.SemaphoreType.DMA
    strip = (CHUNKS, ROWS, LANES)
    wide = (CHUNKS, WIDE, LANES)
    padded = (CHUNKS + 2, WIDE, LANES)
    pieces = len(GATHER_PARTS)
    out = jax.ShapeDtypeStruct((1, ROWS, 2048), F32)
    return pl.pallas_call(
        kernel,
        out_shape=(out, out),
        in_specs=[any_space] * 6,
        out_specs=(any_space, any_space),
        scratch_shapes=[
            pltpu.VMEM((16, ROWS, 2048), BF16),
            pltpu.VMEM((2048, 2048), BF16),
            pltpu.VMEM((PHASES, 16, 2, ROWS, LANES), BF16),
            pltpu.VMEM((PHASES,) + strip, BF16),
            pltpu.VMEM((PHASES,) + strip, BF16),
            pltpu.VMEM((4, 2) + strip, BF16),
            pltpu.VMEM((4, 3, 2, CHUNKS // 2, 2 * HALO, LANES), BF16),
            pltpu.VMEM((5,) + strip, BF16),
            pltpu.VMEM((4, 2, CHUNKS // 2, 2 * HALO, LANES), BF16),
            pltpu.VMEM(padded, F32),
            pltpu.VMEM(padded, F32),
            pltpu.VMEM(padded, F32),
            pltpu.VMEM(wide, F32),
            pltpu.VMEM(strip, F32),
            pltpu.VMEM(strip, F32),
            pltpu.VMEM(strip, F32),
            pltpu.VMEM(strip, F32),
            pltpu.VMEM(strip, F32),
            pltpu.VMEM((1024, LANES), F32),
            pltpu.VMEM((ROWS, 2048), F32),
            pltpu.VMEM((4, 4, ROWS, LANES), BF16),
            pltpu.VMEM((4, 4, ROWS, LANES), BF16),
            dma((6,)),
            dma((pieces * 19,)),
            dma((pieces * 32,)),
            dma((16,)),
            dma((32,)),
            dma((PHASES, 16)),
            dma((PHASES, 16)),
            dma((PHASES, 4)),
            dma((PHASES, 4)),
            dma((PHASES, 16)),
            dma((PHASES, 16)),
            dma((4, 8)),
            dma((4, 8)),
            dma((4, 6)),
            dma((4, 6)),
            dma((2,)),
        ],
        compiler_params=pltpu.CompilerParams(
            collective_id=0, has_side_effects=True, vmem_limit_bytes=48 * 2**20
        ),
    )(forcing, mult_start, incr_start, diffusivity, north_corr, east_corr)


def solution(mesh):
    rows = P("sub", "strip", None)
    return jax.shard_map(
        local,
        mesh=mesh,
        in_specs=(rows, rows, rows, rows, P("strip", None), P()),
        out_specs=(rows, rows),
        check_vma=False,
    )
```

```python
import functools

import jax
import jax.numpy as jnp
from jax import lax
from jax.experimental import pallas as pl
from jax.experimental.pallas import tpu as pltpu
from jax.sharding import PartitionSpec as P

STEPS = 4
ITERS = 2
PHASES = ITERS + 1
MESH = pl.DeviceIdType.MESH
F32, BF16 = jnp.float32, jnp.bfloat16

ROWS, WIDE, CHUNKS, LANES = 64, 80, 16, 128
HALO = 8
GATHER_PARTS = ((0, 768, "zy"), (768, 512, "yz"), (1280, 768, "yzx"))

DIFF, INCR, MULT = 0, 1, 2


def kernel(forcing, mult_in, incr_in, diff_in, north, east, mult_out, grad_out,
           north_all, east_all, low_land, half_land, half_mine, strip_land, rim_land, strip_mine, rim_mine,
           work, diff_prev, diff_own, incr_prev, incr_own, mult, force, model, grad_kept, north_sum, east_sum, relay_out, relay_in,
           load_sem, gather_send, gather_recv, shared_send, shared_recv, there_send, there_recv, core_send, core_recv, back_send, back_recv,
           swap_send, swap_recv, relay_send, relay_recv, out_sem):
    sub, strip = lax.axis_index("sub"), lax.axis_index("strip")
    x, z_hi = lax.rem(sub, 4), lax.div(sub, 4)
    y, z, core = lax.div(strip, 8), lax.rem(lax.div(strip, 2), 4), lax.rem(strip, 2)
    chip, z_all = y * 4 + z, z_hi * 4 + z

    def device(x_at, y_at, z_at):
        return (lax.div(z_at, 4) * 4 + x_at, y_at * 8 + lax.rem(z_at, 4) * 2 + core)

    def along(dim, step):
        if dim == "y":
            return device(x, lax.rem(y + step + 4, 4), z_all)
        return device(x, y, lax.rem(z_all + step + 8, 8))

    peer = (sub, strip + 1 - 2 * core)

    def plane(offset):
        to = lax.rem(chip + offset, 16)
        return to, (sub, to * 2 + core)

    def remote(src, dst, send, recv, to):
        return pltpu.make_async_remote_copy(
            src_ref=src, dst_ref=dst, send_sem=send, recv_sem=recv, device_id=to, device_id_type=MESH
        )

    first, last = sub == 0, sub == 7
    top, bottom = strip == 0, strip == 31
    hub = jnp.where(z_hi == 0, 3, 4)
    is_hub = sub == hub
    across = (lax.rem(sub + 4, 8), strip)

    rim_land[...] = jnp.zeros_like(rim_land)
    for ref in (work, diff_prev, diff_own):
        ref[0] = jnp.zeros((WIDE, LANES), F32)
        ref[CHUNKS + 1] = jnp.zeros((WIDE, LANES), F32)

    barrier = pltpu.get_barrier_semaphore()

    def greet(to):
        pl.semaphore_signal(barrier, inc=1, device_id=to, device_id_type=MESH)

    for offset in range(1, 16):
        greet(plane(offset)[1])
    greet(peer)
    greet(across)
    for step in (-2, -1, 1, 2):
        greet(along("z", step))
    for step in (-1, 1):
        greet(device(lax.rem(x + step + 4, 4), y, z_all))
    near = [
        (-1, 0, ~first), (1, 0, ~last),
        (-1, -1, ~first & ~top), (-1, 1, ~first & ~bottom),
        (1, -1, ~last & ~top), (1, 1, ~last & ~bottom),
        (0, -1, ~top), (0, 1, ~bottom),
    ]
    for d_sub, d_strip, there in near:
        @pl.when(there)
        def _(d_sub=d_sub, d_strip=d_strip):
            greet((sub + d_sub, strip + d_strip))
    for part in range(4):
        @pl.when(is_hub & (x != part))
        def _(part=part):
            greet((z_hi * 4 + part, strip))

    @pl.when(~is_hub)
    def _():
        greet((hub, strip))

    expected = 23 + jnp.where(is_hub, 3, 1)
    for _, _, there in near:
        expected = expected + there.astype(jnp.int32)
    def load(source, target, sem):
        for j in range(CHUNKS):
            pltpu.make_async_copy(source.at[:, pl.ds(LANES * j, LANES)], target.at[j], sem).start()

    def loaded(target, sem):
        pltpu.make_async_copy(target, target, sem).wait()

    load(mult_in.at[0], mult, load_sem.at[0])
    load(incr_in.at[0], incr_own, load_sem.at[1])
    load(diff_in.at[0], force, load_sem.at[2])
    shared = GATHER_PARTS[2][0]
    own_rows = pl.ds(pl.multiple_of(16 * x, 16), 16)
    own_north = [
        pltpu.make_async_copy(north.at[:, pl.ds(0, shared)], north_all.at[chip, :, pl.ds(0, shared)], load_sem.at[3]),
        pltpu.make_async_copy(
            north.at[own_rows, pl.ds(shared, 2048 - shared)],
            north_all.at[chip, own_rows, pl.ds(shared, 2048 - shared)], load_sem.at[5]),
    ]
    for copy in own_north:
        copy.start()
    own_east = pltpu.make_async_copy(east, east_all, load_sem.at[4])
    own_east.start()
    pl.semaphore_wait(barrier, expected)

    gather_sends = []

    def gather_copy(part, piece, half, source, to, recv_at, sends):
        start, size, order = GATHER_PARTS[part]
        if half is not None:
            width = size // 2 // LANES * LANES
            start, size = (start, width) if half == 0 else (start + width, size - width)
        columns = pl.ds(start, size)
        rows = pl.ds(pl.multiple_of(16 * x, 16), 16) if "x" in order else pl.ds(0, ROWS)
        source = source.at[rows, columns] if source is north else source.at[piece, rows, columns]
        return remote(source, north_all.at[piece, rows, columns], gather_send.at[sends], gather_recv.at[recv_at], to)

    def slot(part, rel_a, rel_b, half):
        return ((part * 4 + rel_a) * 4 + rel_b) * 2 + (half or 0)

    def piece_of(part, rel_a, rel_b):
        rel_z, rel_y = (rel_a, rel_b) if GATHER_PARTS[part][2][0] == "z" else (rel_b, rel_a)
        return lax.rem(y + rel_y, 4) * 4 + lax.rem(z + rel_z, 4)

    def gather_put(part, rel_a, rel_b, ring, step, half=None):
        to_a, to_b = ((rel_a - step) % 4, rel_b) if ring == 0 else (rel_a, (rel_b - step) % 4)
        copy = gather_copy(
            part, piece_of(part, rel_a, rel_b), half, north if (rel_a, rel_b) == (0, 0) else north_all,
            along(GATHER_PARTS[part][2][ring], step), slot(part, to_a, to_b, half), len(gather_sends),
        )
        copy.start()
        gather_sends.append(copy)

    def gather_wait(part, rel_a, rel_b, half=None):
        gather_copy(part, piece_of(part, rel_a, rel_b), half, north_all, peer, slot(part, rel_a, rel_b, half), 0).wait_recv()

    parts = range(len(GATHER_PARTS))

    def gather_start():
        for part in parts:
            gather_put(part, 0, 0, 0, 1)
            gather_put(part, 0, 0, 0, -1)
        for part in parts:
            gather_put(part, 0, 0, 1, 1)
            gather_put(part, 0, 0, 1, -1)
            gather_put(part, 0, 0, 0, 2)

    def gather_first(rel):
        for part in parts:
            gather_wait(part, rel, 0)
            gather_put(part, rel, 0, 1, 1)
            gather_put(part, rel, 0, 1, -1)

    def gather_second(rel_a):
        for part in parts:
            for rel, step in ((3, 1), (1, -1)):
                gather_wait(part, rel_a, rel)
                gather_put(part, rel_a, rel, 1, step, half=0 if step == 1 else 1)

    def gather_far(rel_a, some):
        for part in some:
            gather_wait(part, rel_a, 2, 0)
            gather_wait(part, rel_a, 2, 1)

    def shared_ref(rel_a, far, half):
        start, size, _ = GATHER_PARTS[2]
        if half is not None:
            start, size = start + half * (size // 2), size // 2
        at = lax.rem(y + rel_a, 4)
        rows = pl.ds(pl.multiple_of(16 * lax.rem(x + far, 4), 16), 16)
        return north_all.at[pl.ds(4 * at, 4), rows, pl.ds(start, size)]

    def shared_put(rel_a, far, step, half=None):
        ref = shared_ref(rel_a, far, half)
        at = (rel_a * 4 + (far - step) % 4) * 2 + (half or 0)
        copy = remote(ref, ref, shared_send.at[len(shared_sends)], shared_recv.at[at],
                      device(lax.rem(x + step + 4, 4), y, z_all))
        copy.start()
        shared_sends.append(copy)

    def shared_wait(rel_a, far, half=None):
        ref = shared_ref(rel_a, far, half)
        at = (rel_a * 4 + far) * 2 + (half or 0)
        remote(ref, ref, shared_recv.at[at], shared_recv.at[at], peer).wait_recv()

    shared_sends = []

    def shared_start(rel_a):
        for _ in parts[:1]:
            shared_put(rel_a, 0, 1)
            shared_put(rel_a, 0, -1)

    def shared_on(rel_a):
        for _ in parts[:1]:
            shared_wait(rel_a, 3)
            shared_put(rel_a, 3, 1, half=0)
            shared_wait(rel_a, 1)
            shared_put(rel_a, 1, -1, half=1)

    def shared_end(rel_a):
        for _ in parts[:1]:
            shared_wait(rel_a, 2, 0)
            shared_wait(rel_a, 2, 1)

    gather_start()

    def swap_copies(which):
        copies = []
        for at, d_sub in ((0, 1), (1, -1)):
            if which < MULT and d_sub == -1:
                continue
            sent = ~last & (sub != 3) if d_sub == 1 else ~first & (sub != 4)
            heard = ~first & (sub != 4) if d_sub == 1 else ~last & (sub != 3)
            copies.append((remote(
                strip_mine.at[which], strip_land.at[which, at], swap_send.at[which, at],
                swap_recv.at[which, at], (sub + d_sub, strip)), sent, heard))
        for at, d_sub in ((0, 1), (1, 0), (2, -1)):
            if (which == INCR and d_sub == 0) or (which < MULT and d_sub == -1):
                continue
            sub_sent = {1: ~last, 0: first | ~first, -1: ~first}[d_sub]
            sub_heard = {1: ~first, 0: first | ~first, -1: ~last}[d_sub]
            for edge, d_strip in ((0, -1), (1, 1)):
                sent = sub_sent & (~top if d_strip == -1 else ~bottom)
                heard = sub_heard & (~bottom if d_strip == -1 else ~top)
                number = 2 + 2 * at + edge
                copies.append((remote(
                    rim_mine.at[which, edge], rim_land.at[which, at, 1 - edge], swap_send.at[which, number],
                    swap_recv.at[which, number], (sub + d_sub, strip + d_strip)), sent, heard))
        return copies

    def swap_start(which):
        relay_from_hub(which)
        for copy, sent, _ in swap_copies(which):
            pl.when(sent)(copy.start)

    def swap_wait_number(which, numbers):
        copies = swap_copies(which)
        order = ([0, 1] if which >= MULT else [0]) + [
            2 + 2 * at + edge
            for at, d_sub in ((0, 1), (1, 0), (2, -1))
            if not ((which == INCR and d_sub == 0) or (which < MULT and d_sub == -1))
            for edge in (0, 1)
        ]
        for number, (copy, _, heard) in zip(order, copies, strict=True):
            if number in numbers:
                pl.when(heard)(copy.wait_recv)

    def relay_copies(which):
        up_only = which < MULT
        gives = z_hi == 0 if up_only else z_hi >= 0
        takes = z_hi == 1 if up_only else z_hi >= 0
        land = 0 if up_only else jnp.where(z_hi == 0, 1, 0)
        far_land = 0 if up_only else 1 - land
        quarter = lambda ref, part: ref.at[pl.ds(4 * part, 4)]
        send, recv = relay_send.at[which], relay_recv.at[which]
        outward = [
            (remote(quarter(strip_mine.at[which], part), relay_out.at[which], send.at[part], recv.at[0],
                    (z_hi * 4 + part, strip)), gives & is_hub & (x != part))
            for part in range(4)
        ]
        mine, kept = quarter(strip_mine.at[which], x), relay_out.at[which]
        there, there_kept = quarter(strip_land.at[which, far_land], x), relay_in.at[which]
        far_hub = across[0] == 7 - hub
        over = [
            (remote(mine, there_kept, send.at[4], recv.at[1], across), gives & is_hub),
            (remote(kept, there, send.at[4], recv.at[1], across), gives & ~is_hub & far_hub),
            (remote(kept, there_kept, send.at[4], recv.at[1], across), gives & ~is_hub & ~far_hub),
        ]
        inward = (remote(relay_in.at[which], quarter(strip_land.at[which, land], x), send.at[5], recv.at[2 + x], (hub, strip)),
                  takes & ~is_hub)
        waits = {
            "out": (outward[0][0], gives & ~is_hub),
            "over": (over[0][0], takes),
            "in": [
                (remote(relay_in.at[which], quarter(strip_land.at[which, land], part), send.at[5], recv.at[2 + part], (hub, strip)),
                 takes & is_hub & (x != part))
                for part in range(4)
            ],
        }
        return outward, over, inward, waits

    def relay_from_hub(which):
        outward, over, _, _ = relay_copies(which)
        pl.when(over[0][1])(over[0][0].start)
        for copy, sent in outward:
            pl.when(sent)(copy.start)

    def relay_across(which):
        _, over, _, waits = relay_copies(which)
        copy, heard = waits["out"]
        pl.when(heard)(copy.wait_recv)
        for copy, sent in over[1:]:
            pl.when(sent)(copy.start)

    def relay_to_hub(which):
        _, _, (copy, sent), waits = relay_copies(which)
        arrived, heard = waits["over"]
        pl.when(heard)(arrived.wait_recv)
        pl.when(sent)(copy.start)

    def relay_end(which, hub_sub):
        for copy, heard in relay_copies(which)[3]["in"]:
            pl.when(heard & (sub == hub_sub))(copy.wait_recv)

    def relay_sent(which):
        outward, over, (copy, sent), _ = relay_copies(which)
        for one, was in outward:
            pl.when(was)(one.wait_send)
        gives = over[0][1] | over[1][1] | over[2][1]
        pl.when(gives)(over[0][0].wait_send)
        pl.when(sent)(copy.wait_send)

    FROM_BEFORE, FROM_SAME, FROM_AFTER = (0, 2, 3), (4, 5), (1, 6, 7)

    def pack(which, field):
        for pair in range(CHUNKS // 2):
            left, right = field[2 * pair], field[2 * pair + 1]
            if which < MULT:
                strip_mine[which, 2 * pair] = left.astype(BF16)
                strip_mine[which, 2 * pair + 1] = right.astype(BF16)
            rim_mine[which, 0, pair] = jnp.concatenate([left[:HALO], right[:HALO]], axis=0).astype(BF16)
            rim_mine[which, 1, pair] = jnp.concatenate([left[-HALO:], right[-HALO:]], axis=0).astype(BF16)

    def widened(which, source, chunk_rows, pair):
        above = rim_land[which, source, 0, pair].astype(F32)
        below = rim_land[which, source, 1, pair].astype(F32)
        return [
            jnp.concatenate(
                [above[h * HALO:(h + 1) * HALO], chunk_rows(2 * pair + h), below[h * HALO:(h + 1) * HALO]], axis=0
            )
            for h in (0, 1)
        ]

    def each_wide(which, source, chunk_rows, put):
        for pair in range(CHUNKS // 2):
            for h, value in enumerate(widened(which, source, chunk_rows, pair)):
                put(2 * pair + h, value)

    def landed(which, source):
        return lambda j: strip_land[which, source, j].astype(F32)

    lane = lax.broadcasted_iota(jnp.int32, (WIDE, LANES), 1)
    leftmost, rightmost = lane == 0, lane == LANES - 1

    def spread(before, now, now_left, after_left):
        now_right = pltpu.roll(now, 1, 1)
        total = (
            jnp.where(leftmost, before, now_right) + jnp.where(rightmost, after_left, now_left)
            + pltpu.roll(now, 1, 0) + pltpu.roll(now, WIDE - 1, 0) - 4.0 * now
        )
        return total, now_right

    def run_steps(diff, adjoint):
        nothing = jnp.zeros((WIDE, LANES), F32)

        @pl.loop(0, STEPS)
        def _(step):
            field = work[1]
            before, now = nothing, diff[1] * field if adjoint else field
            now_left = pltpu.roll(now, LANES - 1, 1)
            for j in range(1, CHUNKS + 1):
                later = after = after_left = nothing
                if j < CHUNKS:
                    later = work[j + 1]
                    after = diff[j + 1] * later if adjoint else later
                    after_left = pltpu.roll(after, LANES - 1, 1)
                total, now_right = spread(before, now, now_left, after_left)
                work[j] = field + total if adjoint else now + diff[j] * total
                before, now, now_left, field = now_right, after, after_left, later

    def put_work(j, value):
        work[j + 1] = value

    row = lax.broadcasted_iota(jnp.int32, (WIDE, LANES), 0)
    inside = ~((row < HALO) & top) & ~((row >= HALO + ROWS) & bottom)

    low_of = (4, MULT, MULT + 1)

    def chip_at(to):
        return (sub, to * 2 + core)

    def apart(low, high):
        return lax.rem(high - low + 16, 16)

    def there_copy(phase, to):
        at = apart(chip, to)
        return remote(strip_mine.at[low_of[phase], to], low_land.at[phase, chip, core],
                      there_send.at[phase, at], there_recv.at[phase, at], chip_at(to))

    def there_own(phase):
        low_land[phase, chip, core] = strip_mine[low_of[phase], chip]

    def core_copy(phase, row):
        mine = low_land.at[phase, pl.ds(4 * row, 4), core]
        at = lax.rem(row - y + 4, 4)
        return remote(mine, mine, core_send.at[phase, at], core_recv.at[phase, at], peer)

    def back_copy(phase, to):
        at = apart(chip, to)
        return remote(half_mine.at[phase, to], half_land.at[phase, chip],
                      back_send.at[phase, at], back_recv.at[phase, at], chip_at(to))

    def from_row(make, recv, phase, d_row):
        row = lax.rem(y + d_row, 4)
        for d_z in range(1 if d_row == 0 else 0, 4):
            source = row * 4 + lax.rem(z + d_z, 4)
            copy = make(phase, source)
            at = apart(source, chip)
            remote(copy.src_ref, copy.dst_ref, recv.at[phase, at], recv.at[phase, at], peer).wait_recv()
        return row

    ORDER = (0, 1, 3, 2)

    def north_product(phase, when_heard=lambda: None):
        rows = []

        def arrive(d_row):
            row = from_row(there_copy, there_recv, phase, d_row)
            core_copy(phase, row).start()
            rows.append(row)

        def columns(row):
            return low_land[phase, pl.ds(4 * row, 4)].reshape(4 * 2 * ROWS, LANES)

        arrive(ORDER[0])
        for number in range(4):
            if number < 3:
                arrive(ORDER[number + 1])
            if number == 2:
                when_heard()
            row = rows[number]
            core_copy(phase, row).wait_recv()
            depth = pl.ds(pl.multiple_of(512 * row, 512), 512)
            if number < 3:
                product = jnp.dot(
                    north_all[:, :, depth].reshape(1024, 512), columns(row), preferred_element_type=F32)
                north_sum[...] = product if number == 0 else north_sum[...] + product
                continue
            for d_row in (2, 1, 3, 0):
                to_row = lax.rem(y + d_row, 4)
                part = pl.ds(pl.multiple_of(256 * to_row, 256), 256)
                product = jnp.dot(
                    north_all[pl.ds(4 * to_row, 4), :, depth].reshape(256, 512), columns(row),
                    preferred_element_type=F32)
                half = (north_sum[part, :] + product).astype(BF16).reshape(4, ROWS, LANES)
                half_mine[phase, pl.ds(4 * to_row, 4)] = half
                for d_z in range(1 if d_row == 0 else 0, 4):
                    back_copy(phase, to_row * 4 + lax.rem(z + d_z, 4)).start()
        half_land[phase, chip] = half_mine[phase, chip]

    def east_product(phase, finish):
        for number, d_row in enumerate(ORDER):
            row = from_row(back_copy, back_recv, phase, d_row)
            left = jnp.concatenate([half_land[phase, 4 * row + c] for c in range(4)], axis=1)
            depth = pl.ds(pl.multiple_of(512 * row, 512), 512)
            if number < 3:
                product = jnp.dot(left, east_all[depth, :], preferred_element_type=F32)
                east_sum[...] = product if number == 0 else east_sum[...] + product
                continue
            for d_pair in range(8):
                pair = lax.rem(lax.div(chip, 2) + d_pair, 8)
                part = pl.ds(pl.multiple_of(256 * pair, 256), 256)
                product = east_sum[:, part] + jnp.dot(left, east_all[depth, part], preferred_element_type=F32)
                for h in (0, 1):
                    finish(2 * pair + h, product[:, LANES * h:LANES * (h + 1)], d_pair == 0)

    loaded(mult, load_sem.at[0])
    for j in range(CHUNKS):
        strip_mine[4, j] = mult[j].astype(BF16)
    for offset in range(1, 16):
        there_copy(0, plane(offset)[0]).start()
    there_own(0)
    loaded(force, load_sem.at[2])
    pack(DIFF, force)
    loaded(incr_own, load_sem.at[1])
    pack(INCR, incr_own)
    gather_first(3)
    gather_first(1)
    for copy in own_north:
        copy.wait()
    gather_second(0)
    gather_first(2)
    swap_start(DIFF)
    swap_start(INCR)
    gather_second(3)
    gather_second(1)
    gather_far(0, parts[2:])
    shared_start(0)
    gather_second(2)
    relay_across(DIFF)
    relay_across(INCR)
    for rel_a in (3, 1):
        gather_far(rel_a, parts[2:])
        shared_start(rel_a)
    shared_on(0)
    gather_far(2, parts[2:])
    shared_start(2)
    swap_wait_number(DIFF, FROM_SAME)

    def put_own(j, value):
        diff_own[j + 1] = value

    each_wide(DIFF, 1, lambda j: force[j], put_own)
    load(forcing.at[0], force, load_sem.at[2])
    shared_on(3)
    shared_on(1)
    relay_to_hub(DIFF)
    relay_to_hub(INCR)
    shared_on(2)
    for rel_a in (0, 3, 1, 2):
        gather_far(rel_a, parts[:2])
        shared_end(rel_a)
    north_product(0)
    swap_wait_number(DIFF, FROM_BEFORE)
    relay_end(DIFF, 4)

    def put_prev(j, value):
        diff_prev[j + 1] = value

    each_wide(DIFF, 0, landed(DIFF, 0), put_prev)
    swap_wait_number(INCR, FROM_BEFORE)
    relay_end(INCR, 4)

    def put_incr(j, value):
        incr_prev[j] = value
        work[j + 1] = value

    each_wide(INCR, 0, landed(INCR, 0), put_incr)
    run_steps(diff_prev, False)
    loaded(force, load_sem.at[2])
    for j in range(CHUNKS):
        model[j] = force[j] - incr_own[j] + jnp.where(first, 0.0, work[j + 1, HALO:HALO + ROWS])
    own_east.wait()

    def update(phase):
        def finish(j, product, own):
            value = mult[j] + 0.5 * (model[j] - product)
            mult[j] = value
            rounded = value.astype(BF16)
            strip_mine[low_of[phase + 1], j] = rounded
            if not own:
                there_copy(phase + 1, j).start()
            else:
                @pl.when(j != chip)
                def _():
                    there_copy(phase + 1, j).start()
        return finish

    east_product(0, update(0))

    for phase in range(1, PHASES):
        which = MULT - 1 + phase
        final = phase == PHASES - 1
        there_own(phase)
        pack(which, mult)
        swap_start(which)
        swap_wait_number(which, FROM_SAME)
        each_wide(which, 1, lambda j: mult[j], put_work)
        run_steps(diff_prev, True)
        for j in range(CHUNKS):
            incr_prev[j] = incr_prev[j] - 0.5 * work[j + 1]
        north_product(phase, lambda: relay_across(which))
        def stored(source, target, j, sem):
            columns = pl.ds(pl.multiple_of(LANES * j, LANES), LANES)
            pltpu.make_async_copy(source, target.at[0, :, columns], sem).start()

        def own_increments():
            swap_wait_number(which, FROM_AFTER)
            relay_end(which, 3)
            each_wide(which, 2, landed(which, 1), put_work)
            run_steps(diff_own, True)
            for j in range(CHUNKS):
                grad = mult[j] - jnp.where(last, 0.0, work[j + 1, HALO:HALO + ROWS])
                incr_own[j] = incr_own[j] + 0.5 * grad
                if final:
                    grad_kept[j] = grad
                    stored(grad_kept.at[j], grad_out, j, out_sem.at[0])

        pl.when(sub != 3)(own_increments)
        relay_to_hub(which)
        swap_wait_number(which, FROM_BEFORE)
        relay_end(which, 4)

        def put_before(j, value):
            value = jnp.where(inside, incr_prev[j] + 0.5 * value, 0.0)
            incr_prev[j] = value
            work[j + 1] = value

        each_wide(which, 0, landed(which, 0), put_before)
        run_steps(diff_prev, False)
        for j in range(CHUNKS):
            model[j] = force[j] + jnp.where(first, 0.0, work[j + 1, HALO:HALO + ROWS])
        pl.when(sub == 3)(own_increments)
        for j in range(CHUNKS):
            model[j] = model[j] - incr_own[j]
        if not final:
            east_product(phase, update(phase))
        else:
            def finish(j, product, own):
                mult[j] = model[j] - product
                stored(mult.at[j], mult_out, j, out_sem.at[1])

            east_product(phase, finish)

    for copy in gather_sends + shared_sends:
        copy.wait_send()
    for phase in range(PHASES):
        for offset in range(1, 16):
            there_copy(phase, plane(offset)[0]).wait_send()
            back_copy(phase, plane(offset)[0]).wait_send()
        for row in range(4):
            core_copy(phase, row).wait_send()
    for which in (DIFF, INCR, MULT, MULT + 1):
        for copy, sent, _ in swap_copies(which):
            pl.when(sent)(copy.wait_send)
        relay_sent(which)
    pltpu.make_async_copy(model, model, out_sem.at[0]).wait()
    pltpu.make_async_copy(model, model, out_sem.at[1]).wait()


def local(forcing, mult_start, incr_start, diffusivity, north_corr, east_corr):
    any_space = pl.BlockSpec(memory_space=pltpu.HBM)
    dma = pltpu.SemaphoreType.DMA
    strip = (CHUNKS, ROWS, LANES)
    wide = (CHUNKS, WIDE, LANES)
    padded = (CHUNKS + 2, WIDE, LANES)
    pieces = len(GATHER_PARTS)
    out = jax.ShapeDtypeStruct((1, ROWS, 2048), F32)
    return pl.pallas_call(
        kernel,
        out_shape=(out, out),
        in_specs=[any_space] * 6,
        out_specs=(any_space, any_space),
        scratch_shapes=[
            pltpu.VMEM((16, ROWS, 2048), BF16),
            pltpu.VMEM((2048, 2048), BF16),
            pltpu.VMEM((PHASES, 16, 2, ROWS, LANES), BF16),
            pltpu.VMEM((PHASES,) + strip, BF16),
            pltpu.VMEM((PHASES,) + strip, BF16),
            pltpu.VMEM((4, 2) + strip, BF16),
            pltpu.VMEM((4, 3, 2, CHUNKS // 2, 2 * HALO, LANES), BF16),
            pltpu.VMEM((5,) + strip, BF16),
            pltpu.VMEM((4, 2, CHUNKS // 2, 2 * HALO, LANES), BF16),
            pltpu.VMEM(padded, F32),
            pltpu.VMEM(padded, F32),
            pltpu.VMEM(padded, F32),
            pltpu.VMEM(wide, F32),
            pltpu.VMEM(strip, F32),
            pltpu.VMEM(strip, F32),
            pltpu.VMEM(strip, F32),
            pltpu.VMEM(strip, F32),
            pltpu.VMEM(strip, F32),
            pltpu.VMEM((1024, LANES), F32),
            pltpu.VMEM((ROWS, 2048), F32),
            pltpu.VMEM((4, 4, ROWS, LANES), BF16),
            pltpu.VMEM((4, 4, ROWS, LANES), BF16),
            dma((6,)),
            dma((pieces * 19,)),
            dma((pieces * 32,)),
            dma((16,)),
            dma((32,)),
            dma((PHASES, 16)),
            dma((PHASES, 16)),
            dma((PHASES, 4)),
            dma((PHASES, 4)),
            dma((PHASES, 16)),
            dma((PHASES, 16)),
            dma((4, 8)),
            dma((4, 8)),
            dma((4, 6)),
            dma((4, 6)),
            dma((2,)),
        ],
        compiler_params=pltpu.CompilerParams(
            collective_id=0, has_side_effects=True, vmem_limit_bytes=60 * 2**20
        ),
    )(forcing, mult_start, incr_start, diffusivity, north_corr, east_corr)


def solution(mesh):
    rows = P("sub", "strip", None)
    return jax.shard_map(
        local,
        mesh=mesh,
        in_specs=(rows, rows, rows, rows, P("strip", None), P()),
        out_specs=(rows, rows),
        check_vma=False,
    )
```

```python
import functools

import jax
import jax.numpy as jnp
from jax import lax
from jax.experimental import pallas as pl
from jax.experimental.pallas import tpu as pltpu
from jax.sharding import PartitionSpec as P

STEPS = 4
ITERS = 2
PHASES = ITERS + 1
MESH = pl.DeviceIdType.MESH
F32, BF16 = jnp.float32, jnp.bfloat16

ROWS, WIDE, CHUNKS, LANES = 64, 80, 16, 128
HALO = 8
GATHER_PARTS = ((0, 1024, "zy"), (1024, 1024, "yz"))

DIFF, INCR, MULT = 0, 1, 2


def kernel(forcing, mult_in, incr_in, diff_in, north, east, mult_out, grad_out,
           north_all, east_all, low_land, half_land, half_mine, strip_land, rim_land, strip_mine, rim_mine,
           work, diff_prev, diff_own, incr_prev, incr_own, mult, force, model, north_sum, east_sum, relay_out, relay_in,
           load_sem, gather_send, gather_recv, there_send, there_recv, core_send, core_recv, back_send, back_recv,
           swap_send, swap_recv, relay_send, relay_recv, out_sem):
    sub, strip = lax.axis_index("sub"), lax.axis_index("strip")
    x, z_hi = lax.rem(sub, 4), lax.div(sub, 4)
    y, z, core = lax.div(strip, 8), lax.rem(lax.div(strip, 2), 4), lax.rem(strip, 2)
    chip, z_all = y * 4 + z, z_hi * 4 + z

    def device(x_at, y_at, z_at):
        return (lax.div(z_at, 4) * 4 + x_at, y_at * 8 + lax.rem(z_at, 4) * 2 + core)

    def along(dim, step):
        if dim == "y":
            return device(x, lax.rem(y + step + 4, 4), z_all)
        return device(x, y, lax.rem(z_all + step + 8, 8))

    peer = (sub, strip + 1 - 2 * core)

    def plane(offset):
        to = lax.rem(chip + offset, 16)
        return to, (sub, to * 2 + core)

    def remote(src, dst, send, recv, to):
        return pltpu.make_async_remote_copy(
            src_ref=src, dst_ref=dst, send_sem=send, recv_sem=recv, device_id=to, device_id_type=MESH
        )

    first, last = sub == 0, sub == 7
    top, bottom = strip == 0, strip == 31
    hub = jnp.where(z_hi == 0, 3, 4)
    is_hub = sub == hub
    across = (lax.rem(sub + 4, 8), strip)

    rim_land[...] = jnp.zeros_like(rim_land)

    barrier = pltpu.get_barrier_semaphore()

    def greet(to):
        pl.semaphore_signal(barrier, inc=1, device_id=to, device_id_type=MESH)

    for offset in range(1, 16):
        greet(plane(offset)[1])
    greet(peer)
    greet(across)
    for step in (-1, 1):
        greet(along("z", step))
    near = [
        (-1, 0, ~first), (1, 0, ~last),
        (-1, -1, ~first & ~top), (-1, 1, ~first & ~bottom),
        (1, -1, ~last & ~top), (1, 1, ~last & ~bottom),
        (0, -1, ~top), (0, 1, ~bottom),
    ]
    for d_sub, d_strip, there in near:
        @pl.when(there)
        def _(d_sub=d_sub, d_strip=d_strip):
            greet((sub + d_sub, strip + d_strip))
    for part in range(4):
        @pl.when(is_hub & (x != part))
        def _(part=part):
            greet((z_hi * 4 + part, strip))

    @pl.when(~is_hub)
    def _():
        greet((hub, strip))

    expected = 19 + jnp.where(is_hub, 3, 1)
    for _, _, there in near:
        expected = expected + there.astype(jnp.int32)
    def load(source, target, sem):
        for j in range(CHUNKS):
            pltpu.make_async_copy(source.at[:, pl.ds(LANES * j, LANES)], target.at[j], sem).start()

    def loaded(target, sem):
        pltpu.make_async_copy(target, target, sem).wait()

    own_north = pltpu.make_async_copy(north, north_all.at[chip], load_sem.at[3])
    own_north.start()
    load(mult_in.at[0], mult, load_sem.at[0])
    load(incr_in.at[0], incr_own, load_sem.at[1])
    load(diff_in.at[0], force, load_sem.at[2])
    own_east = pltpu.make_async_copy(east, east_all, load_sem.at[4])
    own_east.start()

    pl.semaphore_wait(barrier, expected)

    gather_sends = []

    def part_copy(part, piece, half, to, recv_at, sends):
        start, size, _ = GATHER_PARTS[part]
        if half is not None:
            start, size = start + half * (size // 2), size // 2
        columns = pl.ds(start, size)
        return remote(north_all.at[piece, :, columns], north_all.at[piece, :, columns], gather_send.at[sends], gather_recv.at[recv_at], to)

    def slot(part, rel_a, rel_b, half=0):
        return ((part * 4 + rel_a) * 4 + rel_b) * 2 + half

    def piece_of(part, rel_a, rel_b):
        rel_z, rel_y = (rel_a, rel_b) if GATHER_PARTS[part][2] == "zy" else (rel_b, rel_a)
        return lax.rem(y + rel_y, 4) * 4 + lax.rem(z + rel_z, 4)

    def gather_send_piece(part, rel_a, rel_b, dim_at, step, half=None):
        dim = GATHER_PARTS[part][2][dim_at]
        to_a, to_b = (rel_a, rel_b)
        if dim_at == 0:
            to_a = (rel_a - step) % 4
        else:
            to_b = (rel_b - step) % 4
        copy = part_copy(
            part, piece_of(part, rel_a, rel_b), half, along(dim, step),
            slot(part, to_a, to_b, half or 0), len(gather_sends),
        )
        copy.start()
        gather_sends.append(copy)

    def gather_wait(part, rel_a, rel_b, half=None):
        part_copy(part, piece_of(part, rel_a, rel_b), half, peer, slot(part, rel_a, rel_b, half or 0), 0).wait_recv()

    parts = range(len(GATHER_PARTS))
    own_north.wait()
    for part in parts:
        for dim_at in (0, 1):
            for step in (1, -1):
                gather_send_piece(part, 0, 0, dim_at, step)

    def gather_first_ring():
        for rel, step in ((3, 1), (1, -1)):
            for part in parts:
                gather_wait(part, rel, 0)
                gather_send_piece(part, rel, 0, 0, step, half=0 if step == 1 else 1)
                gather_send_piece(part, rel, 0, 1, 1)
                gather_send_piece(part, rel, 0, 1, -1)

    def gather_own_second():
        for rel, step in ((3, 1), (1, -1)):
            for part in parts:
                gather_wait(part, 0, rel)
                gather_send_piece(part, 0, rel, 1, step, half=0 if step == 1 else 1)

    def gather_far():
        for part in parts:
            gather_wait(part, 2, 0, 0)
            gather_wait(part, 2, 0, 1)
            gather_send_piece(part, 2, 0, 1, 1)
            gather_send_piece(part, 2, 0, 1, -1)

    def gather_rest(which):
        for rel_a in which:
            for rel, step in ((3, 1), (1, -1)):
                for part in parts:
                    gather_wait(part, rel_a, rel)
                    gather_send_piece(part, rel_a, rel, 1, step, half=0 if step == 1 else 1)

    def gather_row(d_row):
        pieces = [(1, d_row, 2)] + ([(0, rel_a, 2) for rel_a in range(4)] if d_row == 2 else [])
        for part, rel_a, rel_b in pieces:
            gather_wait(part, rel_a, rel_b, 0)
            gather_wait(part, rel_a, rel_b, 1)

    def swap_copies(which):
        copies = []
        for at, d_sub in ((0, 1), (1, -1)):
            if which < MULT and d_sub == -1:
                continue
            sent = ~last & (sub != 3) if d_sub == 1 else ~first & (sub != 4)
            heard = ~first & (sub != 4) if d_sub == 1 else ~last & (sub != 3)
            copies.append((remote(
                strip_mine.at[which], strip_land.at[which, at], swap_send.at[which, at],
                swap_recv.at[which, at], (sub + d_sub, strip)), sent, heard))
        for at, d_sub in ((0, 1), (1, 0), (2, -1)):
            if (which == INCR and d_sub == 0) or (which < MULT and d_sub == -1):
                continue
            sub_sent = {1: ~last, 0: first | ~first, -1: ~first}[d_sub]
            sub_heard = {1: ~first, 0: first | ~first, -1: ~last}[d_sub]
            for edge, d_strip in ((0, -1), (1, 1)):
                sent = sub_sent & (~top if d_strip == -1 else ~bottom)
                heard = sub_heard & (~bottom if d_strip == -1 else ~top)
                number = 2 + 2 * at + edge
                copies.append((remote(
                    rim_mine.at[which, edge], rim_land.at[which, at, 1 - edge], swap_send.at[which, number],
                    swap_recv.at[which, number], (sub + d_sub, strip + d_strip)), sent, heard))
        return copies

    def swap_start(which):
        relay_from_hub(which)
        for copy, sent, _ in swap_copies(which):
            pl.when(sent)(copy.start)

    def swap_wait_number(which, numbers):
        copies = swap_copies(which)
        order = ([0, 1] if which >= MULT else [0]) + [
            2 + 2 * at + edge
            for at, d_sub in ((0, 1), (1, 0), (2, -1))
            if not ((which == INCR and d_sub == 0) or (which < MULT and d_sub == -1))
            for edge in (0, 1)
        ]
        for number, (copy, _, heard) in zip(order, copies, strict=True):
            if number in numbers:
                pl.when(heard)(copy.wait_recv)

    def relay_copies(which):
        up_only = which < MULT
        gives = z_hi == 0 if up_only else z_hi >= 0
        takes = z_hi == 1 if up_only else z_hi >= 0
        land = 0 if up_only else jnp.where(z_hi == 0, 1, 0)
        far_land = 0 if up_only else 1 - land
        quarter = lambda ref, part: ref.at[pl.ds(4 * part, 4)]
        send, recv = relay_send.at[which], relay_recv.at[which]
        outward = [
            (remote(quarter(strip_mine.at[which], part), relay_out.at[which], send.at[part], recv.at[0],
                    (z_hi * 4 + part, strip)), gives & is_hub & (x != part))
            for part in range(4)
        ]
        mine, kept = quarter(strip_mine.at[which], x), relay_out.at[which]
        there, there_kept = quarter(strip_land.at[which, far_land], x), relay_in.at[which]
        far_hub = across[0] == 7 - hub
        over = [
            (remote(mine, there_kept, send.at[4], recv.at[1], across), gives & is_hub),
            (remote(kept, there, send.at[4], recv.at[1], across), gives & ~is_hub & far_hub),
            (remote(kept, there_kept, send.at[4], recv.at[1], across), gives & ~is_hub & ~far_hub),
        ]
        inward = (remote(relay_in.at[which], quarter(strip_land.at[which, land], x), send.at[5], recv.at[2 + x], (hub, strip)),
                  takes & ~is_hub)
        waits = {
            "out": (outward[0][0], gives & ~is_hub),
            "over": (over[0][0], takes),
            "in": [
                (remote(relay_in.at[which], quarter(strip_land.at[which, land], part), send.at[5], recv.at[2 + part], (hub, strip)),
                 takes & is_hub & (x != part))
                for part in range(4)
            ],
        }
        return outward, over, inward, waits

    def relay_from_hub(which):
        outward, over, _, _ = relay_copies(which)
        pl.when(over[0][1])(over[0][0].start)
        for copy, sent in outward:
            pl.when(sent)(copy.start)

    def relay_across(which):
        _, over, _, waits = relay_copies(which)
        copy, heard = waits["out"]
        pl.when(heard)(copy.wait_recv)
        for copy, sent in over[1:]:
            pl.when(sent)(copy.start)

    def relay_to_hub(which):
        _, _, (copy, sent), waits = relay_copies(which)
        arrived, heard = waits["over"]
        pl.when(heard)(arrived.wait_recv)
        pl.when(sent)(copy.start)

    def relay_end(which, hub_sub):
        for copy, heard in relay_copies(which)[3]["in"]:
            pl.when(heard & (sub == hub_sub))(copy.wait_recv)

    def relay_sent(which):
        outward, over, (copy, sent), _ = relay_copies(which)
        for one, was in outward:
            pl.when(was)(one.wait_send)
        gives = over[0][1] | over[1][1] | over[2][1]
        pl.when(gives)(over[0][0].wait_send)
        pl.when(sent)(copy.wait_send)

    FROM_BEFORE, FROM_SAME, FROM_AFTER = (0, 2, 3), (4, 5), (1, 6, 7)

    def pack(which, field):
        for pair in range(CHUNKS // 2):
            left, right = field[2 * pair], field[2 * pair + 1]
            if which < MULT:
                strip_mine[which, 2 * pair] = left.astype(BF16)
                strip_mine[which, 2 * pair + 1] = right.astype(BF16)
            rim_mine[which, 0, pair] = jnp.concatenate([left[:HALO], right[:HALO]], axis=0).astype(BF16)
            rim_mine[which, 1, pair] = jnp.concatenate([left[-HALO:], right[-HALO:]], axis=0).astype(BF16)

    def widened(which, source, chunk_rows, pair):
        above = rim_land[which, source, 0, pair].astype(F32)
        below = rim_land[which, source, 1, pair].astype(F32)
        return [
            jnp.concatenate(
                [above[h * HALO:(h + 1) * HALO], chunk_rows(2 * pair + h), below[h * HALO:(h + 1) * HALO]], axis=0
            )
            for h in (0, 1)
        ]

    def each_wide(which, source, chunk_rows, put):
        for pair in range(CHUNKS // 2):
            for h, value in enumerate(widened(which, source, chunk_rows, pair)):
                put(2 * pair + h, value)

    def landed(which, source):
        return lambda j: strip_land[which, source, j].astype(F32)

    lane = lax.broadcasted_iota(jnp.int32, (WIDE, LANES), 1)
    leftmost, rightmost = lane == 0, lane == LANES - 1

    def spread(before, now, now_left, after_left):
        now_right = pltpu.roll(now, 1, 1)
        total = (
            jnp.where(leftmost, before, now_right) + jnp.where(rightmost, after_left, now_left)
            + pltpu.roll(now, 1, 0) + pltpu.roll(now, WIDE - 1, 0) - 4.0 * now
        )
        return total, now_right

    def run_steps(diff, adjoint):
        nothing = jnp.zeros((WIDE, LANES), F32)

        @pl.loop(0, STEPS)
        def _(step):
            field = work[1]
            before, now = nothing, diff[1] * field if adjoint else field
            now_left = pltpu.roll(now, LANES - 1, 1)
            for j in range(1, CHUNKS + 1):
                later = after = after_left = nothing
                if j < CHUNKS:
                    later = work[j + 1]
                    after = diff[j + 1] * later if adjoint else later
                    after_left = pltpu.roll(after, LANES - 1, 1)
                total, now_right = spread(before, now, now_left, after_left)
                work[j] = field + total if adjoint else now + diff[j] * total
                before, now, now_left, field = now_right, after, after_left, later

    def put_work(j, value):
        work[j + 1] = value

    row = lax.broadcasted_iota(jnp.int32, (WIDE, LANES), 0)
    inside = ~((row < HALO) & top) & ~((row >= HALO + ROWS) & bottom)

    low_of = (4, MULT, MULT + 1)

    def chip_at(to):
        return (sub, to * 2 + core)

    def apart(low, high):
        return lax.rem(high - low + 16, 16)

    def there_copy(phase, to):
        at = apart(chip, to)
        return remote(strip_mine.at[low_of[phase], to], low_land.at[phase, chip, core],
                      there_send.at[phase, at], there_recv.at[phase, at], chip_at(to))

    def there_own(phase):
        low_land[phase, chip, core] = strip_mine[low_of[phase], chip]

    def core_copy(phase, row):
        mine = low_land.at[phase, pl.ds(4 * row, 4), core]
        at = lax.rem(row - y + 4, 4)
        return remote(mine, mine, core_send.at[phase, at], core_recv.at[phase, at], peer)

    def back_copy(phase, to):
        at = apart(chip, to)
        return remote(half_mine.at[phase, to], half_land.at[phase, chip],
                      back_send.at[phase, at], back_recv.at[phase, at], chip_at(to))

    def from_row(make, recv, phase, d_row):
        row = lax.rem(y + d_row, 4)
        for d_z in range(1 if d_row == 0 else 0, 4):
            source = row * 4 + lax.rem(z + d_z, 4)
            copy = make(phase, source)
            at = apart(source, chip)
            remote(copy.src_ref, copy.dst_ref, recv.at[phase, at], recv.at[phase, at], peer).wait_recv()
        return row

    ORDER = (0, 1, 3, 2)

    def half_back(phase, to_row, d_row, product):
        half_mine[phase, pl.ds(4 * to_row, 4)] = product.astype(BF16).reshape(4, ROWS, LANES)
        for d_z in range(1 if d_row == 0 else 0, 4):
            back_copy(phase, to_row * 4 + lax.rem(z + d_z, 4)).start()

    def arrive_all(phase):
        rows = [from_row(there_copy, there_recv, phase, d_row) for d_row in ORDER]
        for row in rows:
            core_copy(phase, row).start()
        return rows

    def north_product(phase):
        rows = []

        def arrive(d_row):
            row = from_row(there_copy, there_recv, phase, d_row)
            core_copy(phase, row).start()
            rows.append(row)

        def columns(row):
            return low_land[phase, pl.ds(4 * row, 4)].reshape(4 * 2 * ROWS, LANES)

        arrive(ORDER[0])
        for number in range(4):
            if number < 3:
                arrive(ORDER[number + 1])
            row = rows[number]
            core_copy(phase, row).wait_recv()
            depth = pl.ds(pl.multiple_of(512 * row, 512), 512)
            if number < 3:
                product = jnp.dot(
                    north_all[:, :, depth].reshape(1024, 512), columns(row), preferred_element_type=F32)
                north_sum[...] = product if number == 0 else north_sum[...] + product
                continue
            for d_row in (2, 1, 3, 0):
                to_row = lax.rem(y + d_row, 4)
                part = pl.ds(pl.multiple_of(256 * to_row, 256), 256)
                product = jnp.dot(
                    north_all[pl.ds(4 * to_row, 4), :, depth].reshape(256, 512), columns(row),
                    preferred_element_type=F32)
                half_back(phase, to_row, d_row, north_sum[part, :] + product)
        half_land[phase, chip] = half_mine[phase, chip]

    def east_product(phase, finish):
        for number, d_row in enumerate(ORDER):
            row = from_row(back_copy, back_recv, phase, d_row)
            left = jnp.concatenate([half_land[phase, 4 * row + c] for c in range(4)], axis=1)
            depth = pl.ds(pl.multiple_of(512 * row, 512), 512)
            if number < 3:
                product = jnp.dot(left, east_all[depth, :], preferred_element_type=F32)
                east_sum[...] = product if number == 0 else east_sum[...] + product
                continue
            for d_pair in range(8):
                pair = lax.rem(lax.div(chip, 2) + d_pair, 8)
                part = pl.ds(pl.multiple_of(256 * pair, 256), 256)
                product = east_sum[:, part] + jnp.dot(left, east_all[depth, part], preferred_element_type=F32)
                for h in (0, 1):
                    finish(2 * pair + h, product[:, LANES * h:LANES * (h + 1)], d_pair == 0)

    loaded(mult, load_sem.at[0])
    for j in range(CHUNKS):
        strip_mine[4, j] = mult[j].astype(BF16)
    for offset in range(1, 16):
        there_copy(0, plane(offset)[0]).start()
    there_own(0)
    loaded(force, load_sem.at[2])
    pack(DIFF, force)
    swap_start(DIFF)
    loaded(incr_own, load_sem.at[1])
    pack(INCR, incr_own)
    swap_start(INCR)
    gather_first_ring()
    gather_own_second()
    relay_across(DIFF)
    relay_across(INCR)
    gather_far()
    swap_wait_number(DIFF, FROM_SAME)

    def put_own(j, value):
        diff_own[j + 1] = value

    each_wide(DIFF, 1, lambda j: force[j], put_own)
    load(forcing.at[0], force, load_sem.at[2])
    relay_to_hub(DIFF)
    relay_to_hub(INCR)
    gather_rest((3, 1))
    low_rows = arrive_all(0)
    gather_rest((2,))
    for row in low_rows:
        core_copy(0, row).wait_recv()
    for d_row in (0, 1, 3, 2):
        gather_row(d_row)
        to_row = lax.rem(y + d_row, 4)
        half_back(0, to_row, d_row, jnp.dot(
            north_all[pl.ds(4 * to_row, 4)].reshape(256, 2048), low_land[0].reshape(2048, LANES),
            preferred_element_type=F32))
    half_land[0, chip] = half_mine[0, chip]
    swap_wait_number(DIFF, FROM_BEFORE)
    relay_end(DIFF, 4)

    def put_prev(j, value):
        diff_prev[j + 1] = value

    each_wide(DIFF, 0, landed(DIFF, 0), put_prev)
    swap_wait_number(INCR, FROM_BEFORE)
    relay_end(INCR, 4)

    def put_incr(j, value):
        incr_prev[j] = value
        work[j + 1] = value

    each_wide(INCR, 0, landed(INCR, 0), put_incr)
    run_steps(diff_prev, False)
    loaded(force, load_sem.at[2])
    for j in range(CHUNKS):
        model[j] = force[j] - incr_own[j] + jnp.where(first, 0.0, work[j + 1, HALO:HALO + ROWS])
    own_east.wait()

    def update(phase):
        def finish(j, product, own):
            value = mult[j] + 0.5 * (model[j] - product)
            mult[j] = value
            rounded = value.astype(BF16)
            strip_mine[low_of[phase + 1], j] = rounded
            if not own:
                there_copy(phase + 1, j).start()
            else:
                @pl.when(j != chip)
                def _():
                    there_copy(phase + 1, j).start()
        return finish

    east_product(0, update(0))

    for phase in range(1, PHASES):
        which = MULT - 1 + phase
        final = phase == PHASES - 1
        there_own(phase)
        pack(which, mult)
        swap_start(which)
        swap_wait_number(which, FROM_SAME)
        each_wide(which, 1, lambda j: mult[j], put_work)
        relay_across(which)
        run_steps(diff_prev, True)
        for j in range(CHUNKS):
            incr_prev[j] = incr_prev[j] - 0.5 * work[j + 1]
        north_product(phase)
        relay_to_hub(which)
        swap_wait_number(which, FROM_BEFORE)
        relay_end(which, 4)

        def put_before(j, value):
            value = jnp.where(inside, incr_prev[j] + 0.5 * value, 0.0)
            incr_prev[j] = value
            work[j + 1] = value

        each_wide(which, 0, landed(which, 0), put_before)
        run_steps(diff_prev, False)
        for j in range(CHUNKS):
            model[j] = force[j] + jnp.where(first, 0.0, work[j + 1, HALO:HALO + ROWS])
        swap_wait_number(which, FROM_AFTER)
        relay_end(which, 3)
        each_wide(which, 2, landed(which, 1), put_work)
        run_steps(diff_own, True)

        def stored(source, target, j, sem):
            columns = pl.ds(pl.multiple_of(LANES * j, LANES), LANES)
            pltpu.make_async_copy(source, target.at[0, :, columns], sem).start()

        for j in range(CHUNKS):
            grad = mult[j] - jnp.where(last, 0.0, work[j + 1, HALO:HALO + ROWS])
            incr = incr_own[j] + 0.5 * grad
            incr_own[j] = incr
            model[j] = model[j] - incr
            if final:
                force[j] = grad
                stored(force.at[j], grad_out, j, out_sem.at[0])

        if not final:
            east_product(phase, update(phase))
        else:
            def finish(j, product, own):
                mult[j] = model[j] - product
                stored(mult.at[j], mult_out, j, out_sem.at[1])

            east_product(phase, finish)

    for copy in gather_sends:
        copy.wait_send()
    for phase in range(PHASES):
        for offset in range(1, 16):
            there_copy(phase, plane(offset)[0]).wait_send()
            back_copy(phase, plane(offset)[0]).wait_send()
        for row in range(4):
            core_copy(phase, row).wait_send()
    for which in (DIFF, INCR, MULT, MULT + 1):
        for copy, sent, _ in swap_copies(which):
            pl.when(sent)(copy.wait_send)
        relay_sent(which)
    pltpu.make_async_copy(model, model, out_sem.at[0]).wait()
    pltpu.make_async_copy(model, model, out_sem.at[1]).wait()


def local(forcing, mult_start, incr_start, diffusivity, north_corr, east_corr):
    any_space = pl.BlockSpec(memory_space=pltpu.HBM)
    dma = pltpu.SemaphoreType.DMA
    strip = (CHUNKS, ROWS, LANES)
    wide = (CHUNKS, WIDE, LANES)
    padded = (CHUNKS + 2, WIDE, LANES)
    pieces = len(GATHER_PARTS)
    out = jax.ShapeDtypeStruct((1, ROWS, 2048), F32)
    return pl.pallas_call(
        kernel,
        out_shape=(out, out),
        in_specs=[any_space] * 6,
        out_specs=(any_space, any_space),
        scratch_shapes=[
            pltpu.VMEM((16, ROWS, 2048), BF16),
            pltpu.VMEM((2048, 2048), BF16),
            pltpu.VMEM((PHASES, 16, 2, ROWS, LANES), BF16),
            pltpu.VMEM((PHASES,) + strip, BF16),
            pltpu.VMEM((PHASES,) + strip, BF16),
            pltpu.VMEM((4, 2) + strip, BF16),
            pltpu.VMEM((4, 3, 2, CHUNKS // 2, 2 * HALO, LANES), BF16),
            pltpu.VMEM((5,) + strip, BF16),
            pltpu.VMEM((4, 2, CHUNKS // 2, 2 * HALO, LANES), BF16),
            pltpu.VMEM(padded, F32),
            pltpu.VMEM(padded, F32),
            pltpu.VMEM(padded, F32),
            pltpu.VMEM(wide, F32),
            pltpu.VMEM(strip, F32),
            pltpu.VMEM(strip, F32),
            pltpu.VMEM(strip, F32),
            pltpu.VMEM(strip, F32),
            pltpu.VMEM((1024, LANES), F32),
            pltpu.VMEM((ROWS, 2048), F32),
            pltpu.VMEM((4, 4, ROWS, LANES), BF16),
            pltpu.VMEM((4, 4, ROWS, LANES), BF16),
            dma((5,)),
            dma((pieces * 20,)),
            dma((pieces * 32,)),
            dma((PHASES, 16)),
            dma((PHASES, 16)),
            dma((PHASES, 4)),
            dma((PHASES, 4)),
            dma((PHASES, 16)),
            dma((PHASES, 16)),
            dma((4, 8)),
            dma((4, 8)),
            dma((4, 6)),
            dma((4, 6)),
            dma((2,)),
        ],
        compiler_params=pltpu.CompilerParams(
            collective_id=0, has_side_effects=True, vmem_limit_bytes=60 * 2**20
        ),
    )(forcing, mult_start, incr_start, diffusivity, north_corr, east_corr)


def solution(mesh):
    rows = P("sub", "strip", None)
    return jax.shard_map(
        local,
        mesh=mesh,
        in_specs=(rows, rows, rows, rows, P("strip", None), P()),
        out_specs=(rows, rows),
        check_vma=False,
    )
```

```python
import functools

import jax
import jax.numpy as jnp
from jax import lax
from jax.experimental import pallas as pl
from jax.experimental.pallas import tpu as pltpu
from jax.sharding import PartitionSpec as P

STEPS = 4
ITERS = 2
PHASES = ITERS + 1
MESH = pl.DeviceIdType.MESH
F32, BF16 = jnp.float32, jnp.bfloat16

ROWS, WIDE, CHUNKS, LANES = 64, 80, 16, 128
HALO = 8
GATHER_PARTS = ((0, 1280, "zy"), (1280, 768, "yz"))

DIFF, INCR, MULT = 0, 1, 2


def kernel(forcing, mult_in, incr_in, diff_in, north, east, mult_out, grad_out,
           north_all, east_all, low_land, half_land, half_mine, strip_land, rim_land, strip_mine, rim_mine,
           work, diff_prev, diff_own, incr_prev, incr_own, mult, force, model, north_sum, east_sum, relay_out, relay_in,
           load_sem, gather_send, gather_recv, there_send, there_recv, core_send, core_recv, back_send, back_recv,
           swap_send, swap_recv, relay_send, relay_recv, out_sem):
    sub, strip = lax.axis_index("sub"), lax.axis_index("strip")
    x, z_hi = lax.rem(sub, 4), lax.div(sub, 4)
    y, z, core = lax.div(strip, 8), lax.rem(lax.div(strip, 2), 4), lax.rem(strip, 2)
    chip, z_all = y * 4 + z, z_hi * 4 + z

    def device(x_at, y_at, z_at):
        return (lax.div(z_at, 4) * 4 + x_at, y_at * 8 + lax.rem(z_at, 4) * 2 + core)

    def along(dim, step):
        if dim == "y":
            return device(x, lax.rem(y + step + 4, 4), z_all)
        return device(x, y, lax.rem(z_all + step + 8, 8))

    peer = (sub, strip + 1 - 2 * core)

    def plane(offset):
        to = lax.rem(chip + offset, 16)
        return to, (sub, to * 2 + core)

    def remote(src, dst, send, recv, to):
        return pltpu.make_async_remote_copy(
            src_ref=src, dst_ref=dst, send_sem=send, recv_sem=recv, device_id=to, device_id_type=MESH
        )

    first, last = sub == 0, sub == 7
    top, bottom = strip == 0, strip == 31
    hub = jnp.where(z_hi == 0, 3, 4)
    is_hub = sub == hub
    across = (lax.rem(sub + 4, 8), strip)

    rim_land[...] = jnp.zeros_like(rim_land)

    barrier = pltpu.get_barrier_semaphore()

    def greet(to):
        pl.semaphore_signal(barrier, inc=1, device_id=to, device_id_type=MESH)

    for offset in range(1, 16):
        greet(plane(offset)[1])
    greet(peer)
    greet(across)
    for step in (-1, 1):
        greet(along("z", step))
    near = [
        (-1, 0, ~first), (1, 0, ~last),
        (-1, -1, ~first & ~top), (-1, 1, ~first & ~bottom),
        (1, -1, ~last & ~top), (1, 1, ~last & ~bottom),
        (0, -1, ~top), (0, 1, ~bottom),
    ]
    for d_sub, d_strip, there in near:
        @pl.when(there)
        def _(d_sub=d_sub, d_strip=d_strip):
            greet((sub + d_sub, strip + d_strip))
    for part in range(4):
        @pl.when(is_hub & (x != part))
        def _(part=part):
            greet((z_hi * 4 + part, strip))

    @pl.when(~is_hub)
    def _():
        greet((hub, strip))

    expected = 19 + jnp.where(is_hub, 3, 1)
    for _, _, there in near:
        expected = expected + there.astype(jnp.int32)
    def load(source, target, sem):
        for j in range(CHUNKS):
            pltpu.make_async_copy(source.at[:, pl.ds(LANES * j, LANES)], target.at[j], sem).start()

    def loaded(target, sem):
        pltpu.make_async_copy(target, target, sem).wait()

    own_north = pltpu.make_async_copy(north, north_all.at[chip], load_sem.at[3])
    own_north.start()
    load(mult_in.at[0], mult, load_sem.at[0])
    load(incr_in.at[0], incr_own, load_sem.at[1])
    load(diff_in.at[0], force, load_sem.at[2])
    own_east = pltpu.make_async_copy(east, east_all, load_sem.at[4])
    own_east.start()

    pl.semaphore_wait(barrier, expected)

    gather_sends = []

    def part_copy(part, piece, half, to, recv_at, sends):
        start, size, _ = GATHER_PARTS[part]
        if half is not None:
            start, size = start + half * (size // 2), size // 2
        columns = pl.ds(start, size)
        return remote(north_all.at[piece, :, columns], north_all.at[piece, :, columns], gather_send.at[sends], gather_recv.at[recv_at], to)

    def slot(part, rel_a, rel_b, half=0):
        return ((part * 4 + rel_a) * 4 + rel_b) * 2 + half

    def piece_of(part, rel_a, rel_b):
        rel_z, rel_y = (rel_a, rel_b) if GATHER_PARTS[part][2] == "zy" else (rel_b, rel_a)
        return lax.rem(y + rel_y, 4) * 4 + lax.rem(z + rel_z, 4)

    def gather_send_piece(part, rel_a, rel_b, dim_at, step, half=None):
        dim = GATHER_PARTS[part][2][dim_at]
        to_a, to_b = (rel_a, rel_b)
        if dim_at == 0:
            to_a = (rel_a - step) % 4
        else:
            to_b = (rel_b - step) % 4
        copy = part_copy(
            part, piece_of(part, rel_a, rel_b), half, along(dim, step),
            slot(part, to_a, to_b, half or 0), len(gather_sends),
        )
        copy.start()
        gather_sends.append(copy)

    def gather_wait(part, rel_a, rel_b, half=None):
        part_copy(part, piece_of(part, rel_a, rel_b), half, peer, slot(part, rel_a, rel_b, half or 0), 0).wait_recv()

    parts = range(len(GATHER_PARTS))
    own_north.wait()
    for part in parts:
        for dim_at in (0, 1):
            for step in (1, -1):
                gather_send_piece(part, 0, 0, dim_at, step)

    def gather_first_ring():
        for rel, step in ((3, 1), (1, -1)):
            for part in parts:
                gather_wait(part, rel, 0)
                gather_send_piece(part, rel, 0, 0, step, half=0 if step == 1 else 1)
                gather_send_piece(part, rel, 0, 1, 1)
                gather_send_piece(part, rel, 0, 1, -1)

    def gather_own_second():
        for rel, step in ((3, 1), (1, -1)):
            for part in parts:
                gather_wait(part, 0, rel)
                gather_send_piece(part, 0, rel, 1, step, half=0 if step == 1 else 1)

    def gather_far():
        for part in parts:
            gather_wait(part, 2, 0, 0)
            gather_wait(part, 2, 0, 1)
            gather_send_piece(part, 2, 0, 1, 1)
            gather_send_piece(part, 2, 0, 1, -1)

    def gather_rest(which):
        for rel_a in which:
            for rel, step in ((3, 1), (1, -1)):
                for part in parts:
                    gather_wait(part, rel_a, rel)
                    gather_send_piece(part, rel_a, rel, 1, step, half=0 if step == 1 else 1)

    def gather_row(d_row):
        pieces = [(1, d_row, 2)] + ([(0, rel_a, 2) for rel_a in range(4)] if d_row == 2 else [])
        for part, rel_a, rel_b in pieces:
            gather_wait(part, rel_a, rel_b, 0)
            gather_wait(part, rel_a, rel_b, 1)

    def swap_copies(which):
        copies = []
        for at, d_sub in ((0, 1), (1, -1)):
            if which < MULT and d_sub == -1:
                continue
            sent = ~last & (sub != 3) if d_sub == 1 else ~first & (sub != 4)
            heard = ~first & (sub != 4) if d_sub == 1 else ~last & (sub != 3)
            copies.append((remote(
                strip_mine.at[which], strip_land.at[which, at], swap_send.at[which, at],
                swap_recv.at[which, at], (sub + d_sub, strip)), sent, heard))
        for at, d_sub in ((0, 1), (1, 0), (2, -1)):
            if (which == INCR and d_sub == 0) or (which < MULT and d_sub == -1):
                continue
            sub_sent = {1: ~last, 0: first | ~first, -1: ~first}[d_sub]
            sub_heard = {1: ~first, 0: first | ~first, -1: ~last}[d_sub]
            for edge, d_strip in ((0, -1), (1, 1)):
                sent = sub_sent & (~top if d_strip == -1 else ~bottom)
                heard = sub_heard & (~bottom if d_strip == -1 else ~top)
                number = 2 + 2 * at + edge
                copies.append((remote(
                    rim_mine.at[which, edge], rim_land.at[which, at, 1 - edge], swap_send.at[which, number],
                    swap_recv.at[which, number], (sub + d_sub, strip + d_strip)), sent, heard))
        return copies

    def swap_start(which):
        relay_from_hub(which)
        for copy, sent, _ in swap_copies(which):
            pl.when(sent)(copy.start)

    def swap_wait_number(which, numbers):
        copies = swap_copies(which)
        order = ([0, 1] if which >= MULT else [0]) + [
            2 + 2 * at + edge
            for at, d_sub in ((0, 1), (1, 0), (2, -1))
            if not ((which == INCR and d_sub == 0) or (which < MULT and d_sub == -1))
            for edge in (0, 1)
        ]
        for number, (copy, _, heard) in zip(order, copies, strict=True):
            if number in numbers:
                pl.when(heard)(copy.wait_recv)

    def relay_copies(which):
        up_only = which < MULT
        gives = z_hi == 0 if up_only else z_hi >= 0
        takes = z_hi == 1 if up_only else z_hi >= 0
        land = 0 if up_only else jnp.where(z_hi == 0, 1, 0)
        far_land = 0 if up_only else 1 - land
        quarter = lambda ref, part: ref.at[pl.ds(4 * part, 4)]
        send, recv = relay_send.at[which], relay_recv.at[which]
        outward = [
            (remote(quarter(strip_mine.at[which], part), relay_out.at[which], send.at[part], recv.at[0],
                    (z_hi * 4 + part, strip)), gives & is_hub & (x != part))
            for part in range(4)
        ]
        mine, kept = quarter(strip_mine.at[which], x), relay_out.at[which]
        there, there_kept = quarter(strip_land.at[which, far_land], x), relay_in.at[which]
        far_hub = across[0] == 7 - hub
        over = [
            (remote(mine, there_kept, send.at[4], recv.at[1], across), gives & is_hub),
            (remote(kept, there, send.at[4], recv.at[1], across), gives & ~is_hub & far_hub),
            (remote(kept, there_kept, send.at[4], recv.at[1], across), gives & ~is_hub & ~far_hub),
        ]
        inward = (remote(relay_in.at[which], quarter(strip_land.at[which, land], x), send.at[5], recv.at[2 + x], (hub, strip)),
                  takes & ~is_hub)
        waits = {
            "out": (outward[0][0], gives & ~is_hub),
            "over": (over[0][0], takes),
            "in": [
                (remote(relay_in.at[which], quarter(strip_land.at[which, land], part), send.at[5], recv.at[2 + part], (hub, strip)),
                 takes & is_hub & (x != part))
                for part in range(4)
            ],
        }
        return outward, over, inward, waits

    def relay_from_hub(which):
        outward, over, _, _ = relay_copies(which)
        pl.when(over[0][1])(over[0][0].start)
        for copy, sent in outward:
            pl.when(sent)(copy.start)

    def relay_across(which):
        _, over, _, waits = relay_copies(which)
        copy, heard = waits["out"]
        pl.when(heard)(copy.wait_recv)
        for copy, sent in over[1:]:
            pl.when(sent)(copy.start)

    def relay_to_hub(which):
        _, _, (copy, sent), waits = relay_copies(which)
        arrived, heard = waits["over"]
        pl.when(heard)(arrived.wait_recv)
        pl.when(sent)(copy.start)

    def relay_end(which, hub_sub):
        for copy, heard in relay_copies(which)[3]["in"]:
            pl.when(heard & (sub == hub_sub))(copy.wait_recv)

    def relay_sent(which):
        outward, over, (copy, sent), _ = relay_copies(which)
        for one, was in outward:
            pl.when(was)(one.wait_send)
        gives = over[0][1] | over[1][1] | over[2][1]
        pl.when(gives)(over[0][0].wait_send)
        pl.when(sent)(copy.wait_send)

    FROM_BEFORE, FROM_SAME, FROM_AFTER = (0, 2, 3), (4, 5), (1, 6, 7)

    def pack(which, field):
        for pair in range(CHUNKS // 2):
            left, right = field[2 * pair], field[2 * pair + 1]
            if which < MULT:
                strip_mine[which, 2 * pair] = left.astype(BF16)
                strip_mine[which, 2 * pair + 1] = right.astype(BF16)
            rim_mine[which, 0, pair] = jnp.concatenate([left[:HALO], right[:HALO]], axis=0).astype(BF16)
            rim_mine[which, 1, pair] = jnp.concatenate([left[-HALO:], right[-HALO:]], axis=0).astype(BF16)

    def widened(which, source, chunk_rows, pair):
        above = rim_land[which, source, 0, pair].astype(F32)
        below = rim_land[which, source, 1, pair].astype(F32)
        return [
            jnp.concatenate(
                [above[h * HALO:(h + 1) * HALO], chunk_rows(2 * pair + h), below[h * HALO:(h + 1) * HALO]], axis=0
            )
            for h in (0, 1)
        ]

    def each_wide(which, source, chunk_rows, put):
        for pair in range(CHUNKS // 2):
            for h, value in enumerate(widened(which, source, chunk_rows, pair)):
                put(2 * pair + h, value)

    def landed(which, source):
        return lambda j: strip_land[which, source, j].astype(F32)

    lane = lax.broadcasted_iota(jnp.int32, (WIDE, LANES), 1)
    leftmost, rightmost = lane == 0, lane == LANES - 1

    def spread(before, now, now_left, after_left):
        now_right = pltpu.roll(now, 1, 1)
        total = (
            jnp.where(leftmost, before, now_right) + jnp.where(rightmost, after_left, now_left)
            + pltpu.roll(now, 1, 0) + pltpu.roll(now, WIDE - 1, 0) - 4.0 * now
        )
        return total, now_right

    def run_steps(diff, adjoint):
        nothing = jnp.zeros((WIDE, LANES), F32)

        @pl.loop(0, STEPS)
        def _(step):
            field = work[1]
            before, now = nothing, diff[1] * field if adjoint else field
            now_left = pltpu.roll(now, LANES - 1, 1)
            for j in range(1, CHUNKS + 1):
                later = after = after_left = nothing
                if j < CHUNKS:
                    later = work[j + 1]
                    after = diff[j + 1] * later if adjoint else later
                    after_left = pltpu.roll(after, LANES - 1, 1)
                total, now_right = spread(before, now, now_left, after_left)
                work[j] = field + total if adjoint else now + diff[j] * total
                before, now, now_left, field = now_right, after, after_left, later

    def put_work(j, value):
        work[j + 1] = value

    row = lax.broadcasted_iota(jnp.int32, (WIDE, LANES), 0)
    inside = ~((row < HALO) & top) & ~((row >= HALO + ROWS) & bottom)

    low_of = (4, MULT, MULT + 1)

    def chip_at(to):
        return (sub, to * 2 + core)

    def apart(low, high):
        return lax.rem(high - low + 16, 16)

    def there_copy(phase, to):
        at = apart(chip, to)
        return remote(strip_mine.at[low_of[phase], to], low_land.at[phase, chip, core],
                      there_send.at[phase, at], there_recv.at[phase, at], chip_at(to))

    def there_own(phase):
        low_land[phase, chip, core] = strip_mine[low_of[phase], chip]

    def core_copy(phase, row):
        mine = low_land.at[phase, pl.ds(4 * row, 4), core]
        at = lax.rem(row - y + 4, 4)
        return remote(mine, mine, core_send.at[phase, at], core_recv.at[phase, at], peer)

    def back_copy(phase, to):
        at = apart(chip, to)
        return remote(half_mine.at[phase, to], half_land.at[phase, chip],
                      back_send.at[phase, at], back_recv.at[phase, at], chip_at(to))

    def from_row(make, recv, phase, d_row):
        row = lax.rem(y + d_row, 4)
        for d_z in range(1 if d_row == 0 else 0, 4):
            source = row * 4 + lax.rem(z + d_z, 4)
            copy = make(phase, source)
            at = apart(source, chip)
            remote(copy.src_ref, copy.dst_ref, recv.at[phase, at], recv.at[phase, at], peer).wait_recv()
        return row

    ORDER = (0, 1, 3, 2)

    def half_back(phase, to_row, d_row, product):
        half_mine[phase, pl.ds(4 * to_row, 4)] = product.astype(BF16).reshape(4, ROWS, LANES)
        for d_z in range(1 if d_row == 0 else 0, 4):
            back_copy(phase, to_row * 4 + lax.rem(z + d_z, 4)).start()

    def arrive_all(phase):
        rows = [from_row(there_copy, there_recv, phase, d_row) for d_row in ORDER]
        for row in rows:
            core_copy(phase, row).start()
        return rows

    def north_product(phase):
        rows = []

        def arrive(d_row):
            row = from_row(there_copy, there_recv, phase, d_row)
            core_copy(phase, row).start()
            rows.append(row)

        def columns(row):
            return low_land[phase, pl.ds(4 * row, 4)].reshape(4 * 2 * ROWS, LANES)

        arrive(ORDER[0])
        for number in range(4):
            if number < 3:
                arrive(ORDER[number + 1])
            row = rows[number]
            core_copy(phase, row).wait_recv()
            depth = pl.ds(pl.multiple_of(512 * row, 512), 512)
            if number < 3:
                product = jnp.dot(
                    north_all[:, :, depth].reshape(1024, 512), columns(row), preferred_element_type=F32)
                north_sum[...] = product if number == 0 else north_sum[...] + product
                continue
            for d_row in (2, 1, 3, 0):
                to_row = lax.rem(y + d_row, 4)
                part = pl.ds(pl.multiple_of(256 * to_row, 256), 256)
                product = jnp.dot(
                    north_all[pl.ds(4 * to_row, 4), :, depth].reshape(256, 512), columns(row),
                    preferred_element_type=F32)
                half_back(phase, to_row, d_row, north_sum[part, :] + product)
        half_land[phase, chip] = half_mine[phase, chip]

    def east_product(phase, finish):
        for number, d_row in enumerate(ORDER):
            row = from_row(back_copy, back_recv, phase, d_row)
            left = jnp.concatenate([half_land[phase, 4 * row + c] for c in range(4)], axis=1)
            depth = pl.ds(pl.multiple_of(512 * row, 512), 512)
            if number < 3:
                product = jnp.dot(left, east_all[depth, :], preferred_element_type=F32)
                east_sum[...] = product if number == 0 else east_sum[...] + product
                continue
            for d_pair in range(8):
                pair = lax.rem(lax.div(chip, 2) + d_pair, 8)
                part = pl.ds(pl.multiple_of(256 * pair, 256), 256)
                product = east_sum[:, part] + jnp.dot(left, east_all[depth, part], preferred_element_type=F32)
                for h in (0, 1):
                    finish(2 * pair + h, product[:, LANES * h:LANES * (h + 1)], d_pair == 0)

    loaded(mult, load_sem.at[0])
    for j in range(CHUNKS):
        strip_mine[4, j] = mult[j].astype(BF16)
    for offset in range(1, 16):
        there_copy(0, plane(offset)[0]).start()
    there_own(0)
    loaded(force, load_sem.at[2])
    pack(DIFF, force)
    loaded(incr_own, load_sem.at[1])
    pack(INCR, incr_own)
    gather_first_ring()
    gather_own_second()
    gather_far()
    swap_start(DIFF)
    swap_start(INCR)
    gather_rest((3, 1))
    low_rows = arrive_all(0)
    relay_across(DIFF)
    relay_across(INCR)
    swap_wait_number(DIFF, FROM_SAME)

    def put_own(j, value):
        diff_own[j + 1] = value

    each_wide(DIFF, 1, lambda j: force[j], put_own)
    load(forcing.at[0], force, load_sem.at[2])
    gather_rest((2,))
    relay_to_hub(DIFF)
    relay_to_hub(INCR)
    for row in low_rows:
        core_copy(0, row).wait_recv()
    for d_row in (0, 1, 3, 2):
        gather_row(d_row)
        to_row = lax.rem(y + d_row, 4)
        half_back(0, to_row, d_row, jnp.dot(
            north_all[pl.ds(4 * to_row, 4)].reshape(256, 2048), low_land[0].reshape(2048, LANES),
            preferred_element_type=F32))
    half_land[0, chip] = half_mine[0, chip]
    swap_wait_number(DIFF, FROM_BEFORE)
    relay_end(DIFF, 4)

    def put_prev(j, value):
        diff_prev[j + 1] = value

    each_wide(DIFF, 0, landed(DIFF, 0), put_prev)
    swap_wait_number(INCR, FROM_BEFORE)
    relay_end(INCR, 4)

    def put_incr(j, value):
        incr_prev[j] = value
        work[j + 1] = value

    each_wide(INCR, 0, landed(INCR, 0), put_incr)
    run_steps(diff_prev, False)
    loaded(force, load_sem.at[2])
    for j in range(CHUNKS):
        model[j] = force[j] - incr_own[j] + jnp.where(first, 0.0, work[j + 1, HALO:HALO + ROWS])
    own_east.wait()

    def update(phase):
        def finish(j, product, own):
            value = mult[j] + 0.5 * (model[j] - product)
            mult[j] = value
            rounded = value.astype(BF16)
            strip_mine[low_of[phase + 1], j] = rounded
            if not own:
                there_copy(phase + 1, j).start()
            else:
                @pl.when(j != chip)
                def _():
                    there_copy(phase + 1, j).start()
        return finish

    east_product(0, update(0))

    for phase in range(1, PHASES):
        which = MULT - 1 + phase
        final = phase == PHASES - 1
        there_own(phase)
        pack(which, mult)
        swap_start(which)
        swap_wait_number(which, FROM_SAME)
        each_wide(which, 1, lambda j: mult[j], put_work)
        relay_across(which)
        run_steps(diff_prev, True)
        for j in range(CHUNKS):
            incr_prev[j] = incr_prev[j] - 0.5 * work[j + 1]
        north_product(phase)
        relay_to_hub(which)
        swap_wait_number(which, FROM_BEFORE)
        relay_end(which, 4)

        def put_before(j, value):
            value = jnp.where(inside, incr_prev[j] + 0.5 * value, 0.0)
            incr_prev[j] = value
            work[j + 1] = value

        each_wide(which, 0, landed(which, 0), put_before)
        run_steps(diff_prev, False)
        for j in range(CHUNKS):
            model[j] = force[j] + jnp.where(first, 0.0, work[j + 1, HALO:HALO + ROWS])
        swap_wait_number(which, FROM_AFTER)
        relay_end(which, 3)
        each_wide(which, 2, landed(which, 1), put_work)
        run_steps(diff_own, True)

        def stored(source, target, j, sem):
            columns = pl.ds(pl.multiple_of(LANES * j, LANES), LANES)
            pltpu.make_async_copy(source, target.at[0, :, columns], sem).start()

        for j in range(CHUNKS):
            grad = mult[j] - jnp.where(last, 0.0, work[j + 1, HALO:HALO + ROWS])
            incr = incr_own[j] + 0.5 * grad
            incr_own[j] = incr
            model[j] = model[j] - incr
            if final:
                force[j] = grad
                stored(force.at[j], grad_out, j, out_sem.at[0])

        if not final:
            east_product(phase, update(phase))
        else:
            def finish(j, product, own):
                mult[j] = model[j] - product
                stored(mult.at[j], mult_out, j, out_sem.at[1])

            east_product(phase, finish)

    for copy in gather_sends:
        copy.wait_send()
    for phase in range(PHASES):
        for offset in range(1, 16):
            there_copy(phase, plane(offset)[0]).wait_send()
            back_copy(phase, plane(offset)[0]).wait_send()
        for row in range(4):
            core_copy(phase, row).wait_send()
    for which in (DIFF, INCR, MULT, MULT + 1):
        for copy, sent, _ in swap_copies(which):
            pl.when(sent)(copy.wait_send)
        relay_sent(which)
    pltpu.make_async_copy(model, model, out_sem.at[0]).wait()
    pltpu.make_async_copy(model, model, out_sem.at[1]).wait()


def local(forcing, mult_start, incr_start, diffusivity, north_corr, east_corr):
    any_space = pl.BlockSpec(memory_space=pltpu.HBM)
    dma = pltpu.SemaphoreType.DMA
    strip = (CHUNKS, ROWS, LANES)
    wide = (CHUNKS, WIDE, LANES)
    padded = (CHUNKS + 2, WIDE, LANES)
    pieces = len(GATHER_PARTS)
    out = jax.ShapeDtypeStruct((1, ROWS, 2048), F32)
    return pl.pallas_call(
        kernel,
        out_shape=(out, out),
        in_specs=[any_space] * 6,
        out_specs=(any_space, any_space),
        scratch_shapes=[
            pltpu.VMEM((16, ROWS, 2048), BF16),
            pltpu.VMEM((2048, 2048), BF16),
            pltpu.VMEM((PHASES, 16, 2, ROWS, LANES), BF16),
            pltpu.VMEM((PHASES,) + strip, BF16),
            pltpu.VMEM((PHASES,) + strip, BF16),
            pltpu.VMEM((4, 2) + strip, BF16),
            pltpu.VMEM((4, 3, 2, CHUNKS // 2, 2 * HALO, LANES), BF16),
            pltpu.VMEM((5,) + strip, BF16),
            pltpu.VMEM((4, 2, CHUNKS // 2, 2 * HALO, LANES), BF16),
            pltpu.VMEM(padded, F32),
            pltpu.VMEM(padded, F32),
            pltpu.VMEM(padded, F32),
            pltpu.VMEM(wide, F32),
            pltpu.VMEM(strip, F32),
            pltpu.VMEM(strip, F32),
            pltpu.VMEM(strip, F32),
            pltpu.VMEM(strip, F32),
            pltpu.VMEM((1024, LANES), F32),
            pltpu.VMEM((ROWS, 2048), F32),
            pltpu.VMEM((4, 4, ROWS, LANES), BF16),
            pltpu.VMEM((4, 4, ROWS, LANES), BF16),
            dma((5,)),
            dma((pieces * 20,)),
            dma((pieces * 32,)),
            dma((PHASES, 16)),
            dma((PHASES, 16)),
            dma((PHASES, 4)),
            dma((PHASES, 4)),
            dma((PHASES, 16)),
            dma((PHASES, 16)),
            dma((4, 8)),
            dma((4, 8)),
            dma((4, 6)),
            dma((4, 6)),
            dma((2,)),
        ],
        compiler_params=pltpu.CompilerParams(
            collective_id=0, has_side_effects=True, vmem_limit_bytes=60 * 2**20
        ),
    )(forcing, mult_start, incr_start, diffusivity, north_corr, east_corr)


def solution(mesh):
    rows = P("sub", "strip", None)
    return jax.shard_map(
        local,
        mesh=mesh,
        in_specs=(rows, rows, rows, rows, P("strip", None), P()),
        out_specs=(rows, rows),
        check_vma=False,
    )
```

```python
import functools

import jax
import jax.numpy as jnp
from jax import lax
from jax.experimental import pallas as pl
from jax.experimental.pallas import tpu as pltpu
from jax.sharding import PartitionSpec as P

STEPS = 4
ITERS = 2
PHASES = ITERS + 1
MESH = pl.DeviceIdType.MESH
F32, BF16 = jnp.float32, jnp.bfloat16

ROWS, WIDE, CHUNKS, LANES = 64, 80, 16, 128
HALO = 8
GATHER_PARTS = ((0, 1280, "zy"), (1280, 768, "yz"))

DIFF, INCR, MULT = 0, 1, 2


def kernel(forcing, mult_in, incr_in, diff_in, north, east, mult_out, grad_out,
           north_all, east_all, low_land, half_land, half_mine, strip_land, rim_land, strip_mine, rim_mine,
           work, diff_prev, diff_own, incr_prev, incr_own, mult, force, model, grad_kept, north_sum, east_sum, relay_out, relay_in,
           load_sem, gather_send, gather_recv, there_send, there_recv, core_send, core_recv, back_send, back_recv,
           swap_send, swap_recv, relay_send, relay_recv, out_sem):
    sub, strip = lax.axis_index("sub"), lax.axis_index("strip")
    x, z_hi = lax.rem(sub, 4), lax.div(sub, 4)
    y, z, core = lax.div(strip, 8), lax.rem(lax.div(strip, 2), 4), lax.rem(strip, 2)
    chip, z_all = y * 4 + z, z_hi * 4 + z

    def device(x_at, y_at, z_at):
        return (lax.div(z_at, 4) * 4 + x_at, y_at * 8 + lax.rem(z_at, 4) * 2 + core)

    def along(dim, step):
        if dim == "y":
            return device(x, lax.rem(y + step + 4, 4), z_all)
        return device(x, y, lax.rem(z_all + step + 8, 8))

    peer = (sub, strip + 1 - 2 * core)

    def plane(offset):
        to = lax.rem(chip + offset, 16)
        return to, (sub, to * 2 + core)

    def remote(src, dst, send, recv, to):
        return pltpu.make_async_remote_copy(
            src_ref=src, dst_ref=dst, send_sem=send, recv_sem=recv, device_id=to, device_id_type=MESH
        )

    first, last = sub == 0, sub == 7
    top, bottom = strip == 0, strip == 31
    hub = jnp.where(z_hi == 0, 3, 4)
    is_hub = sub == hub
    across = (lax.rem(sub + 4, 8), strip)

    rim_land[...] = jnp.zeros_like(rim_land)

    barrier = pltpu.get_barrier_semaphore()

    def greet(to):
        pl.semaphore_signal(barrier, inc=1, device_id=to, device_id_type=MESH)

    for offset in range(1, 16):
        greet(plane(offset)[1])
    greet(peer)
    greet(across)
    for step in (-1, 1):
        greet(along("z", step))
    near = [
        (-1, 0, ~first), (1, 0, ~last),
        (-1, -1, ~first & ~top), (-1, 1, ~first & ~bottom),
        (1, -1, ~last & ~top), (1, 1, ~last & ~bottom),
        (0, -1, ~top), (0, 1, ~bottom),
    ]
    for d_sub, d_strip, there in near:
        @pl.when(there)
        def _(d_sub=d_sub, d_strip=d_strip):
            greet((sub + d_sub, strip + d_strip))
    for part in range(4):
        @pl.when(is_hub & (x != part))
        def _(part=part):
            greet((z_hi * 4 + part, strip))

    @pl.when(~is_hub)
    def _():
        greet((hub, strip))

    expected = 19 + jnp.where(is_hub, 3, 1)
    for _, _, there in near:
        expected = expected + there.astype(jnp.int32)
    def load(source, target, sem):
        for j in range(CHUNKS):
            pltpu.make_async_copy(source.at[:, pl.ds(LANES * j, LANES)], target.at[j], sem).start()

    def loaded(target, sem):
        pltpu.make_async_copy(target, target, sem).wait()

    own_north = pltpu.make_async_copy(north, north_all.at[chip], load_sem.at[3])
    own_north.start()
    load(mult_in.at[0], mult, load_sem.at[0])
    load(incr_in.at[0], incr_own, load_sem.at[1])
    load(diff_in.at[0], force, load_sem.at[2])
    own_east = pltpu.make_async_copy(east, east_all, load_sem.at[4])
    own_east.start()

    pl.semaphore_wait(barrier, expected)

    gather_sends = []

    def part_copy(part, piece, half, to, recv_at, sends):
        start, size, _ = GATHER_PARTS[part]
        if half is not None:
            start, size = start + half * (size // 2), size // 2
        columns = pl.ds(start, size)
        return remote(north_all.at[piece, :, columns], north_all.at[piece, :, columns], gather_send.at[sends], gather_recv.at[recv_at], to)

    def slot(part, rel_a, rel_b, half=0):
        return ((part * 4 + rel_a) * 4 + rel_b) * 2 + half

    def piece_of(part, rel_a, rel_b):
        rel_z, rel_y = (rel_a, rel_b) if GATHER_PARTS[part][2] == "zy" else (rel_b, rel_a)
        return lax.rem(y + rel_y, 4) * 4 + lax.rem(z + rel_z, 4)

    def gather_send_piece(part, rel_a, rel_b, dim_at, step, half=None):
        dim = GATHER_PARTS[part][2][dim_at]
        to_a, to_b = (rel_a, rel_b)
        if dim_at == 0:
            to_a = (rel_a - step) % 4
        else:
            to_b = (rel_b - step) % 4
        copy = part_copy(
            part, piece_of(part, rel_a, rel_b), half, along(dim, step),
            slot(part, to_a, to_b, half or 0), len(gather_sends),
        )
        copy.start()
        gather_sends.append(copy)

    def gather_wait(part, rel_a, rel_b, half=None):
        part_copy(part, piece_of(part, rel_a, rel_b), half, peer, slot(part, rel_a, rel_b, half or 0), 0).wait_recv()

    parts = range(len(GATHER_PARTS))
    own_north.wait()
    for part in parts:
        for dim_at in (0, 1):
            for step in (1, -1):
                gather_send_piece(part, 0, 0, dim_at, step)

    def gather_first_ring():
        for rel, step in ((3, 1), (1, -1)):
            for part in parts:
                gather_wait(part, rel, 0)
                gather_send_piece(part, rel, 0, 0, step, half=0 if step == 1 else 1)
                gather_send_piece(part, rel, 0, 1, 1)
                gather_send_piece(part, rel, 0, 1, -1)

    def gather_own_second():
        for rel, step in ((3, 1), (1, -1)):
            for part in parts:
                gather_wait(part, 0, rel)
                gather_send_piece(part, 0, rel, 1, step, half=0 if step == 1 else 1)

    def gather_far():
        for part in parts:
            gather_wait(part, 2, 0, 0)
            gather_wait(part, 2, 0, 1)
            gather_send_piece(part, 2, 0, 1, 1)
            gather_send_piece(part, 2, 0, 1, -1)

    def gather_rest(which):
        for rel_a in which:
            for rel, step in ((3, 1), (1, -1)):
                for part in parts:
                    gather_wait(part, rel_a, rel)
                    gather_send_piece(part, rel_a, rel, 1, step, half=0 if step == 1 else 1)

    def gather_row(d_row):
        pieces = [(1, d_row, 2)] + ([(0, rel_a, 2) for rel_a in range(4)] if d_row == 2 else [])
        for part, rel_a, rel_b in pieces:
            gather_wait(part, rel_a, rel_b, 0)
            gather_wait(part, rel_a, rel_b, 1)

    def swap_copies(which):
        copies = []
        for at, d_sub in ((0, 1), (1, -1)):
            if which < MULT and d_sub == -1:
                continue
            sent = ~last & (sub != 3) if d_sub == 1 else ~first & (sub != 4)
            heard = ~first & (sub != 4) if d_sub == 1 else ~last & (sub != 3)
            copies.append((remote(
                strip_mine.at[which], strip_land.at[which, at], swap_send.at[which, at],
                swap_recv.at[which, at], (sub + d_sub, strip)), sent, heard))
        for at, d_sub in ((0, 1), (1, 0), (2, -1)):
            if (which == INCR and d_sub == 0) or (which < MULT and d_sub == -1):
                continue
            sub_sent = {1: ~last, 0: first | ~first, -1: ~first}[d_sub]
            sub_heard = {1: ~first, 0: first | ~first, -1: ~last}[d_sub]
            for edge, d_strip in ((0, -1), (1, 1)):
                sent = sub_sent & (~top if d_strip == -1 else ~bottom)
                heard = sub_heard & (~bottom if d_strip == -1 else ~top)
                number = 2 + 2 * at + edge
                copies.append((remote(
                    rim_mine.at[which, edge], rim_land.at[which, at, 1 - edge], swap_send.at[which, number],
                    swap_recv.at[which, number], (sub + d_sub, strip + d_strip)), sent, heard))
        return copies

    def swap_start(which):
        copies = swap_copies(which)
        soon = {DIFF: (3, 4), INCR: ()}.get(which, (4, 5))
        for at in soon:
            pl.when(copies[at][1])(copies[at][0].start)
        relay_from_hub(which)
        for at, (copy, sent, _) in enumerate(copies):
            if at not in soon:
                pl.when(sent)(copy.start)

    def swap_wait_number(which, numbers):
        copies = swap_copies(which)
        order = ([0, 1] if which >= MULT else [0]) + [
            2 + 2 * at + edge
            for at, d_sub in ((0, 1), (1, 0), (2, -1))
            if not ((which == INCR and d_sub == 0) or (which < MULT and d_sub == -1))
            for edge in (0, 1)
        ]
        for number, (copy, _, heard) in zip(order, copies, strict=True):
            if number in numbers:
                pl.when(heard)(copy.wait_recv)

    def relay_copies(which):
        up_only = which < MULT
        gives = z_hi == 0 if up_only else z_hi >= 0
        takes = z_hi == 1 if up_only else z_hi >= 0
        land = 0 if up_only else jnp.where(z_hi == 0, 1, 0)
        far_land = 0 if up_only else 1 - land
        quarter = lambda ref, part: ref.at[pl.ds(4 * part, 4)]
        send, recv = relay_send.at[which], relay_recv.at[which]
        outward = [
            (remote(quarter(strip_mine.at[which], part), relay_out.at[which], send.at[part], recv.at[0],
                    (z_hi * 4 + part, strip)), gives & is_hub & (x != part))
            for part in range(4)
        ]
        mine, kept = quarter(strip_mine.at[which], x), relay_out.at[which]
        there, there_kept = quarter(strip_land.at[which, far_land], x), relay_in.at[which]
        far_hub = across[0] == 7 - hub
        over = [
            (remote(mine, there_kept, send.at[4], recv.at[1], across), gives & is_hub),
            (remote(kept, there, send.at[4], recv.at[1], across), gives & ~is_hub & far_hub),
            (remote(kept, there_kept, send.at[4], recv.at[1], across), gives & ~is_hub & ~far_hub),
        ]
        inward = (remote(relay_in.at[which], quarter(strip_land.at[which, land], x), send.at[5], recv.at[2 + x], (hub, strip)),
                  takes & ~is_hub)
        waits = {
            "out": (outward[0][0], gives & ~is_hub),
            "over": (over[0][0], takes),
            "in": [
                (remote(relay_in.at[which], quarter(strip_land.at[which, land], part), send.at[5], recv.at[2 + part], (hub, strip)),
                 takes & is_hub & (x != part))
                for part in range(4)
            ],
        }
        return outward, over, inward, waits

    def relay_from_hub(which):
        outward, over, _, _ = relay_copies(which)
        pl.when(over[0][1])(over[0][0].start)
        for copy, sent in outward:
            pl.when(sent)(copy.start)

    def relay_across(which):
        _, over, _, waits = relay_copies(which)
        copy, heard = waits["out"]
        pl.when(heard)(copy.wait_recv)
        for copy, sent in over[1:]:
            pl.when(sent)(copy.start)

    def relay_to_hub(which):
        _, _, (copy, sent), waits = relay_copies(which)
        arrived, heard = waits["over"]
        pl.when(heard)(arrived.wait_recv)
        pl.when(sent)(copy.start)

    def relay_end(which, hub_sub):
        for copy, heard in relay_copies(which)[3]["in"]:
            pl.when(heard & (sub == hub_sub))(copy.wait_recv)

    def relay_sent(which):
        outward, over, (copy, sent), _ = relay_copies(which)
        for one, was in outward:
            pl.when(was)(one.wait_send)
        gives = over[0][1] | over[1][1] | over[2][1]
        pl.when(gives)(over[0][0].wait_send)
        pl.when(sent)(copy.wait_send)

    FROM_BEFORE, FROM_SAME, FROM_AFTER = (0, 2, 3), (4, 5), (1, 6, 7)

    def pack(which, field):
        for pair in range(CHUNKS // 2):
            left, right = field[2 * pair], field[2 * pair + 1]
            if which < MULT:
                strip_mine[which, 2 * pair] = left.astype(BF16)
                strip_mine[which, 2 * pair + 1] = right.astype(BF16)
            rim_mine[which, 0, pair] = jnp.concatenate([left[:HALO], right[:HALO]], axis=0).astype(BF16)
            rim_mine[which, 1, pair] = jnp.concatenate([left[-HALO:], right[-HALO:]], axis=0).astype(BF16)

    def widened(which, source, chunk_rows, pair):
        above = rim_land[which, source, 0, pair].astype(F32)
        below = rim_land[which, source, 1, pair].astype(F32)
        return [
            jnp.concatenate(
                [above[h * HALO:(h + 1) * HALO], chunk_rows(2 * pair + h), below[h * HALO:(h + 1) * HALO]], axis=0
            )
            for h in (0, 1)
        ]

    def each_wide(which, source, chunk_rows, put):
        for pair in range(CHUNKS // 2):
            for h, value in enumerate(widened(which, source, chunk_rows, pair)):
                put(2 * pair + h, value)

    def landed(which, source):
        return lambda j: strip_land[which, source, j].astype(F32)

    lane = lax.broadcasted_iota(jnp.int32, (WIDE, LANES), 1)
    leftmost, rightmost = lane == 0, lane == LANES - 1

    def spread(before, now, now_left, after_left):
        now_right = pltpu.roll(now, 1, 1)
        total = (
            jnp.where(leftmost, before, now_right) + jnp.where(rightmost, after_left, now_left)
            + pltpu.roll(now, 1, 0) + pltpu.roll(now, WIDE - 1, 0) - 4.0 * now
        )
        return total, now_right

    def run_steps(diff, adjoint):
        nothing = jnp.zeros((WIDE, LANES), F32)

        @pl.loop(0, STEPS)
        def _(step):
            field = work[1]
            before, now = nothing, diff[1] * field if adjoint else field
            now_left = pltpu.roll(now, LANES - 1, 1)
            for j in range(1, CHUNKS + 1):
                later = after = after_left = nothing
                if j < CHUNKS:
                    later = work[j + 1]
                    after = diff[j + 1] * later if adjoint else later
                    after_left = pltpu.roll(after, LANES - 1, 1)
                total, now_right = spread(before, now, now_left, after_left)
                work[j] = field + total if adjoint else now + diff[j] * total
                before, now, now_left, field = now_right, after, after_left, later

    def put_work(j, value):
        work[j + 1] = value

    row = lax.broadcasted_iota(jnp.int32, (WIDE, LANES), 0)
    inside = ~((row < HALO) & top) & ~((row >= HALO + ROWS) & bottom)

    low_of = (4, MULT, MULT + 1)

    def chip_at(to):
        return (sub, to * 2 + core)

    def apart(low, high):
        return lax.rem(high - low + 16, 16)

    def there_copy(phase, to):
        at = apart(chip, to)
        return remote(strip_mine.at[low_of[phase], to], low_land.at[phase, chip, core],
                      there_send.at[phase, at], there_recv.at[phase, at], chip_at(to))

    def there_own(phase):
        low_land[phase, chip, core] = strip_mine[low_of[phase], chip]

    def core_copy(phase, row):
        mine = low_land.at[phase, pl.ds(4 * row, 4), core]
        at = lax.rem(row - y + 4, 4)
        return remote(mine, mine, core_send.at[phase, at], core_recv.at[phase, at], peer)

    def back_copy(phase, to):
        at = apart(chip, to)
        return remote(half_mine.at[phase, to], half_land.at[phase, chip],
                      back_send.at[phase, at], back_recv.at[phase, at], chip_at(to))

    def from_row(make, recv, phase, d_row):
        row = lax.rem(y + d_row, 4)
        for d_z in range(1 if d_row == 0 else 0, 4):
            source = row * 4 + lax.rem(z + d_z, 4)
            copy = make(phase, source)
            at = apart(source, chip)
            remote(copy.src_ref, copy.dst_ref, recv.at[phase, at], recv.at[phase, at], peer).wait_recv()
        return row

    ORDER = (0, 1, 3, 2)

    def half_back(phase, to_row, d_row, product):
        half_mine[phase, pl.ds(4 * to_row, 4)] = product.astype(BF16).reshape(4, ROWS, LANES)
        for d_z in range(1 if d_row == 0 else 0, 4):
            back_copy(phase, to_row * 4 + lax.rem(z + d_z, 4)).start()

    def arrive_all(phase):
        rows = [from_row(there_copy, there_recv, phase, d_row) for d_row in ORDER]
        for row in rows:
            core_copy(phase, row).start()
        return rows

    def north_product(phase):
        rows = []

        def arrive(d_row):
            row = from_row(there_copy, there_recv, phase, d_row)
            core_copy(phase, row).start()
            rows.append(row)

        def columns(row):
            return low_land[phase, pl.ds(4 * row, 4)].reshape(4 * 2 * ROWS, LANES)

        arrive(ORDER[0])
        for number in range(4):
            if number < 3:
                arrive(ORDER[number + 1])
            row = rows[number]
            core_copy(phase, row).wait_recv()
            depth = pl.ds(pl.multiple_of(512 * row, 512), 512)
            if number < 3:
                product = jnp.dot(
                    north_all[:, :, depth].reshape(1024, 512), columns(row), preferred_element_type=F32)
                north_sum[...] = product if number == 0 else north_sum[...] + product
                continue
            for d_row in (2, 1, 3, 0):
                to_row = lax.rem(y + d_row, 4)
                part = pl.ds(pl.multiple_of(256 * to_row, 256), 256)
                product = jnp.dot(
                    north_all[pl.ds(4 * to_row, 4), :, depth].reshape(256, 512), columns(row),
                    preferred_element_type=F32)
                half_back(phase, to_row, d_row, north_sum[part, :] + product)
        half_land[phase, chip] = half_mine[phase, chip]

    def east_product(phase, finish):
        for number, d_row in enumerate(ORDER):
            row = from_row(back_copy, back_recv, phase, d_row)
            left = jnp.concatenate([half_land[phase, 4 * row + c] for c in range(4)], axis=1)
            depth = pl.ds(pl.multiple_of(512 * row, 512), 512)
            if number < 3:
                product = jnp.dot(left, east_all[depth, :], preferred_element_type=F32)
                east_sum[...] = product if number == 0 else east_sum[...] + product
                continue
            for d_pair in range(8):
                pair = lax.rem(lax.div(chip, 2) + d_pair, 8)
                part = pl.ds(pl.multiple_of(256 * pair, 256), 256)
                product = east_sum[:, part] + jnp.dot(left, east_all[depth, part], preferred_element_type=F32)
                for h in (0, 1):
                    finish(2 * pair + h, product[:, LANES * h:LANES * (h + 1)], d_pair == 0)

    loaded(mult, load_sem.at[0])
    for j in range(CHUNKS):
        strip_mine[4, j] = mult[j].astype(BF16)
    for offset in range(1, 16):
        there_copy(0, plane(offset)[0]).start()
    there_own(0)
    loaded(force, load_sem.at[2])
    pack(DIFF, force)
    loaded(incr_own, load_sem.at[1])
    pack(INCR, incr_own)
    gather_first_ring()
    gather_own_second()
    gather_far()
    swap_start(DIFF)
    swap_start(INCR)
    gather_rest((3, 1))
    low_rows = arrive_all(0)
    relay_across(DIFF)
    relay_across(INCR)
    swap_wait_number(DIFF, FROM_SAME)

    def put_own(j, value):
        diff_own[j + 1] = value

    each_wide(DIFF, 1, lambda j: force[j], put_own)
    load(forcing.at[0], force, load_sem.at[2])
    gather_rest((2,))
    relay_to_hub(DIFF)
    relay_to_hub(INCR)
    for row in low_rows:
        core_copy(0, row).wait_recv()
    for d_row in (0, 1, 3, 2):
        gather_row(d_row)
        to_row = lax.rem(y + d_row, 4)
        half_back(0, to_row, d_row, jnp.dot(
            north_all[pl.ds(4 * to_row, 4)].reshape(256, 2048), low_land[0].reshape(2048, LANES),
            preferred_element_type=F32))
    half_land[0, chip] = half_mine[0, chip]
    swap_wait_number(DIFF, FROM_BEFORE)
    relay_end(DIFF, 4)

    def put_prev(j, value):
        diff_prev[j + 1] = value

    each_wide(DIFF, 0, landed(DIFF, 0), put_prev)
    swap_wait_number(INCR, FROM_BEFORE)
    relay_end(INCR, 4)

    def put_incr(j, value):
        incr_prev[j] = value
        work[j + 1] = value

    each_wide(INCR, 0, landed(INCR, 0), put_incr)
    run_steps(diff_prev, False)
    loaded(force, load_sem.at[2])
    for j in range(CHUNKS):
        model[j] = force[j] - incr_own[j] + jnp.where(first, 0.0, work[j + 1, HALO:HALO + ROWS])
    own_east.wait()

    def update(phase):
        def finish(j, product, own):
            value = mult[j] + 0.5 * (model[j] - product)
            mult[j] = value
            rounded = value.astype(BF16)
            strip_mine[low_of[phase + 1], j] = rounded
            if not own:
                there_copy(phase + 1, j).start()
            else:
                @pl.when(j != chip)
                def _():
                    there_copy(phase + 1, j).start()
        return finish

    east_product(0, update(0))

    for phase in range(1, PHASES):
        which = MULT - 1 + phase
        final = phase == PHASES - 1
        there_own(phase)
        pack(which, mult)
        swap_start(which)
        swap_wait_number(which, FROM_SAME)
        each_wide(which, 1, lambda j: mult[j], put_work)
        relay_across(which)
        run_steps(diff_prev, True)
        for j in range(CHUNKS):
            incr_prev[j] = incr_prev[j] - 0.5 * work[j + 1]
        north_product(phase)
        relay_to_hub(which)
        def stored(source, target, j, sem):
            columns = pl.ds(pl.multiple_of(LANES * j, LANES), LANES)
            pltpu.make_async_copy(source, target.at[0, :, columns], sem).start()

        def own_increments():
            swap_wait_number(which, FROM_AFTER)
            relay_end(which, 3)
            each_wide(which, 2, landed(which, 1), put_work)
            run_steps(diff_own, True)
            for j in range(CHUNKS):
                grad = mult[j] - jnp.where(last, 0.0, work[j + 1, HALO:HALO + ROWS])
                incr_own[j] = incr_own[j] + 0.5 * grad
                if final:
                    grad_kept[j] = grad
                    stored(grad_kept.at[j], grad_out, j, out_sem.at[0])

        pl.when(sub != 3)(own_increments)
        swap_wait_number(which, FROM_BEFORE)
        relay_end(which, 4)

        def put_before(j, value):
            value = jnp.where(inside, incr_prev[j] + 0.5 * value, 0.0)
            incr_prev[j] = value
            work[j + 1] = value

        each_wide(which, 0, landed(which, 0), put_before)
        run_steps(diff_prev, False)
        for j in range(CHUNKS):
            model[j] = force[j] + jnp.where(first, 0.0, work[j + 1, HALO:HALO + ROWS])
        pl.when(sub == 3)(own_increments)
        for j in range(CHUNKS):
            model[j] = model[j] - incr_own[j]
        if not final:
            east_product(phase, update(phase))
        else:
            def finish(j, product, own):
                mult[j] = model[j] - product
                stored(mult.at[j], mult_out, j, out_sem.at[1])

            east_product(phase, finish)

    for copy in gather_sends:
        copy.wait_send()
    for phase in range(PHASES):
        for offset in range(1, 16):
            there_copy(phase, plane(offset)[0]).wait_send()
            back_copy(phase, plane(offset)[0]).wait_send()
        for row in range(4):
            core_copy(phase, row).wait_send()
    for which in (DIFF, INCR, MULT, MULT + 1):
        for copy, sent, _ in swap_copies(which):
            pl.when(sent)(copy.wait_send)
        relay_sent(which)
    pltpu.make_async_copy(model, model, out_sem.at[0]).wait()
    pltpu.make_async_copy(model, model, out_sem.at[1]).wait()


def local(forcing, mult_start, incr_start, diffusivity, north_corr, east_corr):
    any_space = pl.BlockSpec(memory_space=pltpu.HBM)
    dma = pltpu.SemaphoreType.DMA
    strip = (CHUNKS, ROWS, LANES)
    wide = (CHUNKS, WIDE, LANES)
    padded = (CHUNKS + 2, WIDE, LANES)
    pieces = len(GATHER_PARTS)
    out = jax.ShapeDtypeStruct((1, ROWS, 2048), F32)
    return pl.pallas_call(
        kernel,
        out_shape=(out, out),
        in_specs=[any_space] * 6,
        out_specs=(any_space, any_space),
        scratch_shapes=[
            pltpu.VMEM((16, ROWS, 2048), BF16),
            pltpu.VMEM((2048, 2048), BF16),
            pltpu.VMEM((PHASES, 16, 2, ROWS, LANES), BF16),
            pltpu.VMEM((PHASES,) + strip, BF16),
            pltpu.VMEM((PHASES,) + strip, BF16),
            pltpu.VMEM((4, 2) + strip, BF16),
            pltpu.VMEM((4, 3, 2, CHUNKS // 2, 2 * HALO, LANES), BF16),
            pltpu.VMEM((5,) + strip, BF16),
            pltpu.VMEM((4, 2, CHUNKS // 2, 2 * HALO, LANES), BF16),
            pltpu.VMEM(padded, F32),
            pltpu.VMEM(padded, F32),
            pltpu.VMEM(padded, F32),
            pltpu.VMEM(wide, F32),
            pltpu.VMEM(strip, F32),
            pltpu.VMEM(strip, F32),
            pltpu.VMEM(strip, F32),
            pltpu.VMEM(strip, F32),
            pltpu.VMEM(strip, F32),
            pltpu.VMEM((1024, LANES), F32),
            pltpu.VMEM((ROWS, 2048), F32),
            pltpu.VMEM((4, 4, ROWS, LANES), BF16),
            pltpu.VMEM((4, 4, ROWS, LANES), BF16),
            dma((5,)),
            dma((pieces * 20,)),
            dma((pieces * 32,)),
            dma((PHASES, 16)),
            dma((PHASES, 16)),
            dma((PHASES, 4)),
            dma((PHASES, 4)),
            dma((PHASES, 16)),
            dma((PHASES, 16)),
            dma((4, 8)),
            dma((4, 8)),
            dma((4, 6)),
            dma((4, 6)),
            dma((2,)),
        ],
        compiler_params=pltpu.CompilerParams(
            collective_id=0, has_side_effects=True, vmem_limit_bytes=60 * 2**20
        ),
    )(forcing, mult_start, incr_start, diffusivity, north_corr, east_corr)


def solution(mesh):
    rows = P("sub", "strip", None)
    return jax.shard_map(
        local,
        mesh=mesh,
        in_specs=(rows, rows, rows, rows, P("strip", None), P()),
        out_specs=(rows, rows),
        check_vma=False,
    )
```
